256 devices in a mesh: group: 16 (over z, core), dev: 16 (over x, y).
Axes of the slice: x: 4, y: 4, z: 8, core: 2. Of those that a mesh axis runs over, the one named last changes fastest.
Arguments:
- tiles: bfloat16 [18432, 5, 128, 128], P(('group', 'dev')), may hold values from 0.00029945374 to 0.029907227
- tile_col: int32 [18432, 5], P(('group', 'dev')), may hold values from 0 to 63
- strip_group: int32 [18432], P(('group', 'dev')), may hold values from 0 to 15, as said below
- strip_slot: int32 [18432], P(('group', 'dev')), may hold values from 0 to 15
- live_count: int32 [256], P(('group', 'dev')), may hold values from 36 to 72, as said below
- omega: bfloat16 [131072, 128], P(('group', 'dev')), may hold values from -40 to 40
- idf: float32 [524288], P(('group', 'dev')), may hold values from 0.4 to 20
Outputs:
- q_basis: float32 [524288, 128], P(('group', 'dev'))
- doc_factor: bfloat16 [128, 131072], P(None, ('group', 'dev'))
The draws below stay inside these ranges and needn't reach their ends.
Inputs may be any that keep to these rules, and one draw needn't show every extreme that they name: `strip_group`: among the 72 strips of one device at most 6 name one group; in every draw one group is named by exactly 6 strips of every device. `live_count`: some device has all 72 strips live.
All inputs are finite; a program needn't handle non-finite values.
Results may differ from the reference program's by a relative error of at most 0.0034.
Values may be sent and summed in bfloat16 or wider, within the bound.
A program may use at most 128 MiB of HBM per device.

```python
import math
import jax
import jax.numpy as jnp
from jax import lax

TILE = 128
SKETCH = 128
RB_DEV = 16
RT = 72
TPI = 5
CAP = 6
CB_G = 64
STRIPS = 18432
TERMS = 524288
DOCS = 131072
N_GROUP = 16
N_DEV = 16
DEVICES = 256


def draw_strip_group(key, part):
    base = jax.random.fold_in(key, 11)
    full_group = jax.random.randint(jax.random.fold_in(base, 1), (), 0, N_GROUP)
    device_keys = jax.random.split(jax.random.fold_in(base, 2), DEVICES)

    def one_device(device_key):
        seat_key, order_key = jax.random.split(device_key)
        seats = jnp.arange((N_GROUP - 1) * CAP, dtype=jnp.int32) // CAP
        seats = jax.random.permutation(seat_key, seats)[:RT - CAP]
        others = seats + (seats >= full_group).astype(jnp.int32)
        labels = jnp.concatenate([jnp.zeros((CAP,), jnp.int32) + full_group, others])
        return jax.random.permutation(order_key, labels)
    return jax.vmap(one_device)(device_keys).reshape(DEVICES * RT).astype(jnp.int32)


def draw_live_count(key, part):
    base = jax.random.fold_in(key, 23)
    counts = jax.random.randint(jax.random.fold_in(base, 1), (DEVICES,), RT // 2, RT + 1)
    busiest = jax.random.randint(jax.random.fold_in(base, 2), (), 0, DEVICES)
    return jnp.where(jnp.arange(DEVICES) == busiest, RT, counts).astype(jnp.int32)


def draw_omega(key, part):
    base = jax.random.fold_in(key, 41)
    col_key, value_key = jax.random.split(base)
    scales = jnp.exp(jax.random.uniform(col_key, (SKETCH,), jnp.float32, 0.0, math.log(10.0)))
    values = jnp.clip(jax.random.normal(value_key, (DOCS, SKETCH), jnp.float32), -4.0, 4.0)
    return (values * scales[None, :]).astype(jnp.bfloat16)


def draw_idf(key, part):
    base = jax.random.fold_in(key, 37)
    position = jnp.arange(TERMS, dtype=jnp.float32) / TERMS
    rough = jnp.exp(jax.random.uniform(base, (TERMS,), jnp.float32, math.log(0.5), math.log(2.0)))
    return (1.0 + 3.0 * position) * rough


def touch_ends(array, stream_key, low, high):
    spot = [jax.random.randint(jax.random.fold_in(stream_key, axis), (), 0, length) for axis, length in enumerate(array.shape)]
    longest = array.shape.index(max(array.shape))
    next_to = spot[:longest] + [(spot[longest] + 1) % array.shape[longest]] + spot[longest + 1:]
    return array.at[tuple(spot)].set(low).at[tuple(next_to)].set(high)


def shard_levels(key, extent, cuts, least, top_value):
    level = 1.0
    for dim, shards_of in cuts:
        steps = jax.random.uniform(jax.random.fold_in(jax.random.fold_in(key, 6), dim), (shards_of,), jnp.float32, least / len(cuts), top_value / len(cuts))
        level = level * jnp.repeat(jnp.exp(steps), extent[dim] // shards_of).reshape((-1,) + (1,) * (len(extent) - 1 - dim))
    return level


def setup_inputs(seed: int = 0) -> dict:
    keys = jax.random.split(jax.random.key(seed), 8)
    return {
        "tiles": jnp.clip(jnp.exp(math.log(0.029907227) - 4.6038955 * jax.random.uniform(keys[0], (STRIPS, TPI, TILE, TILE), jnp.float32) ** shard_levels(keys[0], (STRIPS, TPI, TILE, TILE), ((0, 256),), -0.2, 0.2)), 0.00029945374, 0.029907227).astype(jnp.bfloat16),
        "tile_col": touch_ends(jax.random.randint(keys[1], (STRIPS, TPI), 0, CB_G), jax.random.fold_in(keys[1], 1), 0, CB_G - 1).astype(jnp.int32),
        "strip_group": draw_strip_group(jax.random.fold_in(keys[7], 71), 0),
        "strip_slot": touch_ends(jax.random.randint(keys[3], (STRIPS,), 0, RB_DEV), jax.random.fold_in(keys[3], 1), 0, RB_DEV - 1).astype(jnp.int32),
        "live_count": draw_live_count(jax.random.fold_in(keys[7], 71), 0),
        "omega": draw_omega(jax.random.fold_in(keys[7], 71), 0),
        "idf": draw_idf(jax.random.fold_in(keys[7], 71), 0),
    }


def reference(tiles, tile_col, strip_group, strip_slot, live_count, omega, idf):
    n_devices = N_GROUP * N_DEV
    strip_index = jnp.arange(STRIPS, dtype=jnp.int32)
    holder = strip_index // RT
    band_index = holder % N_DEV
    group_index = holder // N_DEV
    live_mask = (strip_index % RT < live_count[holder]).astype(jnp.float32)
    block_row = ((strip_group * N_DEV + band_index) * RB_DEV + strip_slot).astype(jnp.int32)
    block_col = (group_index[:, None] * CB_G + tile_col).astype(jnp.int32)
    omega_blocks = omega.reshape(DOCS // TILE, TILE, SKETCH)

    def strip_terms(inputs):
        tile_set, col_ids, alive_mask = inputs
        picked = omega_blocks[col_ids].astype(jnp.float32)
        product = jnp.einsum('stij,stjk->sik', tile_set.astype(jnp.float32), picked)
        return product * alive_mask[:, None, None]
    partial_value = lax.map(strip_terms, (tiles.reshape(n_devices, RT, TPI, TILE, TILE), block_col.reshape(n_devices, RT, TPI), live_mask.reshape(n_devices, RT)))
    partial_value = partial_value.reshape(STRIPS, TILE, SKETCH)
    summed = jax.ops.segment_sum(partial_value, block_row, num_segments=TERMS // TILE)
    sketch = summed.reshape(TERMS, SKETCH) * idf[:, None]
    gram_matrix = lax.dot_general(sketch.astype(jnp.float32), sketch.astype(jnp.float32), (((0,), (0,)), ((), ())), precision=lax.Precision.HIGHEST, preferred_element_type=jnp.float32) / TERMS
    lower_factor = jnp.linalg.cholesky(gram_matrix)
    q_basis = jax.scipy.linalg.solve_triangular(lower_factor, sketch.T, lower=True).T
    weighted = (idf[:, None] * q_basis).astype(jnp.bfloat16)
    weighted_blocks = weighted.reshape(TERMS // TILE, TILE, SKETCH)

    def doc_terms(running, inputs):
        tile_set, col_ids, row_ids, alive_mask = inputs
        q_rows = weighted_blocks[row_ids].astype(jnp.float32) * alive_mask[:, None, None]
        contrib = jnp.einsum('sik,stij->stkj', q_rows, tile_set.astype(jnp.float32))
        running = running.at[col_ids.reshape(-1)].add(contrib.reshape(-1, SKETCH, TILE))
        return (running, None)
    initial = jnp.zeros((DOCS // TILE, SKETCH, TILE), jnp.float32)
    running, unused = lax.scan(doc_terms, initial, (tiles.reshape(n_devices, RT, TPI, TILE, TILE), block_col.reshape(n_devices, RT, TPI), block_row.reshape(n_devices, RT), live_mask.reshape(n_devices, RT)))
    doc_factor = jnp.transpose(running, (1, 0, 2)).reshape(SKETCH, DOCS).astype(jnp.bfloat16)
    return (q_basis, doc_factor)
```

```python
import functools

import jax
import jax.numpy as jnp
from jax import lax
from jax.experimental import pallas as pl
from jax.experimental.pallas import tpu as pltpu
from jax.sharding import Mesh
from jax.sharding import PartitionSpec as P

AXES = ("z", "c", "x", "y")
MESH = pl.DeviceIdType.MESH
BF16 = jnp.bfloat16
F32 = jnp.float32
T = 128
NZ = 8
HIGH = lax.Precision.HIGHEST
NT = (((1,), (1,)), ((), ()))
ANY = pl.BlockSpec(memory_space=pl.ANY)
VMEM = pl.BlockSpec(memory_space=pltpu.VMEM)
SMEM = pl.BlockSpec(memory_space=pltpu.SMEM)
MIB = 1 << 20


def place():
    return {a: lax.axis_index(a) for a in AXES}


def moved(at, axis, step, size):
    there = dict(at)
    there[axis] = lax.rem(at[axis] + (step + size), size)
    return tuple(there[a] for a in AXES)


def greet(devices):
    barrier = pltpu.get_barrier_semaphore()
    for device in devices:
        pl.semaphore_signal(barrier, inc=1, device_id=device, device_id_type=MESH)
    pl.semaphore_wait(barrier, len(devices))


def params(mib, cid=None):
    if cid is None:
        return pltpu.CompilerParams(vmem_limit_bytes=mib * MIB)
    return pltpu.CompilerParams(
        vmem_limit_bytes=mib * MIB, collective_id=cid, has_side_effects=True
    )


def omega_kernel(omega_ref, out_ref, send, recv):
    at = place()

    def index(axis, step):
        there = moved(at, axis, step, 4)
        return there[2] * 4 + there[3]

    def index2(first, step1, second, step2):
        there = dict(at)
        there[first] = lax.rem(at[first] + (step1 + 4), 4)
        there[second] = lax.rem(at[second] + (step2 + 4), 4)
        return there["x"] * 4 + there["y"]

    me = at["x"] * 4 + at["y"]
    for b in range(4):
        out_ref[me, b] = omega_ref[b * T : (b + 1) * T, :].T
    greet([moved(at, "x", 1, 4), moved(at, "x", -1, 4), moved(at, "y", 1, 4), moved(at, "y", -1, 4)])

    def copy(i, k, axis, step, dev, lo, n):
        part = out_ref.at[dev, pl.ds(lo, n)]
        return pltpu.make_async_remote_copy(
            src_ref=part,
            dst_ref=part,
            send_sem=send.at[i, k],
            recv_sem=recv.at[i, k],
            device_id=moved(at, axis, step, 4),
            device_id_type=MESH,
        )

    sent = []

    def go(*args):
        c = copy(*args)
        c.start()
        sent.append(c)

    def begin(i, axis, dev, h):
        go(i, 0, axis, 1, dev, 2 * h, 2)
        go(i, 1, axis, -1, dev, 2 * h, 2)

    def got(i, k, axis, dev, lo, n):
        copy(i, k, axis, 1, dev, lo, n).wait_recv()

    turns = ((0, "x", "y"), (1, "y", "x"))
    for h, a, b in turns:
        begin(5 * h, a, me, h)
    for h, a, b in turns:
        begin(5 * h + 1, b, me, h)
    for h, a, b in turns:
        i = 5 * h
        got(i, 0, a, index(a, -1), 2 * h, 2)
        go(i, 2, a, 1, index(a, -1), 2 * h, 1)
        got(i, 1, a, index(a, 1), 2 * h, 2)
        go(i, 3, a, -1, index(a, 1), 2 * h + 1, 1)
    for h, a, b in turns:
        begin(5 * h + 2, b, index(a, -1), h)
        begin(5 * h + 3, b, index(a, 1), h)
    for h, a, b in turns:
        i = 5 * h
        got(i, 2, a, index(a, 2), 2 * h, 1)
        got(i, 3, a, index(a, 2), 2 * h + 1, 1)
        begin(5 * h + 4, b, index(a, 2), h)
    steps = ((1, 0), (2, -1), (3, 1), (4, 2))
    for k, d in steps:
        for h, a, b in turns:
            i = 5 * h + k
            got(i, 0, b, index2(a, d, b, -1), 2 * h, 2)
            go(i, 2, b, 1, index2(a, d, b, -1), 2 * h, 1)
            got(i, 1, b, index2(a, d, b, 1), 2 * h, 2)
            go(i, 3, b, -1, index2(a, d, b, 1), 2 * h + 1, 1)
    for k, d in steps:
        for h, a, b in turns:
            i = 5 * h + k
            got(i, 2, b, index2(a, d, b, 2), 2 * h, 1)
            got(i, 3, b, index2(a, d, b, 2), 2 * h + 1, 1)
    for c in sent:
        c.wait_send()


def gather_omega(omega):
    return pl.pallas_call(
        omega_kernel,
        out_shape=jax.ShapeDtypeStruct((16, 4, T, T), BF16),
        in_specs=[VMEM],
        out_specs=VMEM,
        scratch_shapes=[pltpu.SemaphoreType.DMA((10, 4)), pltpu.SemaphoreType.DMA((10, 4))],
        compiler_params=params(16, 1),
        name="omega_gather",
    )(omega)


STEP = 8


def sketch_kernel(col, group, slot, live, tiles_ref, omega_ref, out_ref, acc):
    step = pl.program_id(0)

    @pl.when(step == 0)
    def _():
        @pl.loop(0, 256)
        def _(i):
            acc[i] = jnp.zeros((T, T), F32)

    @pl.loop(0, STEP, unroll=4)
    def _(i):
        r = step * STEP + i
        tile_row = jnp.concatenate([tiles_ref[i, j] for j in range(5)], axis=1)
        om = jnp.concatenate([omega_ref[col[r, j]] for j in range(5)], axis=1)
        part = lax.dot_general(om, tile_row, NT, preferred_element_type=F32)
        at = group[r] * 16 + slot[r]
        acc[at] += jnp.where(r < live[0], part, 0.0)

    @pl.when(step == pl.num_programs(0) - 1)
    def _():
        @pl.loop(0, 256, unroll=2)
        def _(i):
            out_ref[i] = acc[i].astype(BF16)


def sketch_parts(tiles, tile_col, strip_group, strip_slot, live_count, omega_all):
    strips = tiles.shape[0]
    return pl.pallas_call(
        sketch_kernel,
        out_shape=jax.ShapeDtypeStruct((256, T, T), BF16),
        grid=(strips // STEP,),
        in_specs=[
            SMEM,
            SMEM,
            SMEM,
            SMEM,
            pl.BlockSpec((STEP, 5, T, T), lambda i: (i, 0, 0, 0)),
            pl.BlockSpec((64, T, T), lambda i: (0, 0, 0)),
        ],
        out_specs=pl.BlockSpec((256, T, T), lambda i: (0, 0, 0)),
        scratch_shapes=[pltpu.VMEM((256, T, T), F32)],
        compiler_params=params(52),
        name="sketch",
    )(tile_col, strip_group, strip_slot, live_count, tiles, omega_all)


ORDER = (4, 3, 5, 2, 6, 1, 7, 0)
SUB = 4


def reduce_kernel(
    x_ref, idf_ref, st_ref, wt_ref, gram_ref,
    own, sib, out_r, out_l, in_r, in_l,
    own_sem, sib_send, sib_recv, r_send, r_recv, l_send, l_recv,
):
    at = place()
    sibling = (at["z"], 1 - at["c"], at["x"], at["y"])
    greet([sibling, moved(at, "z", 1, NZ), moved(at, "z", -1, NZ)])
    mine, theirs, slot_of = [], [], {}
    for q, d in enumerate(ORDER):
        slot_of[d] = q
        z = lax.rem(at["z"] + d, NZ)
        a = pltpu.make_async_remote_copy(
            src_ref=x_ref.at[2 * z + 1 - at["c"]],
            dst_ref=sib.at[q],
            send_sem=sib_send.at[q],
            recv_sem=sib_recv.at[q],
            device_id=sibling,
            device_id_type=MESH,
        )
        b = pltpu.make_async_copy(x_ref.at[2 * z + at["c"]], own.at[q], own_sem.at[q])
        a.start()
        b.start()
        mine.append(b)
        theirs.append(a)
    ready = set()

    def need(q):
        if q not in ready:
            ready.add(q)
            mine[q].wait()
            theirs[q].wait_recv()

    sent = []

    def copy(right, s, sub):
        rows = pl.ds(sub * SUB, SUB)
        return pltpu.make_async_remote_copy(
            src_ref=(out_r if right else out_l).at[s, rows],
            dst_ref=(in_r if right else in_l).at[s, rows],
            send_sem=(r_send if right else l_send).at[s, sub],
            recv_sem=(r_recv if right else l_recv).at[s, sub],
            device_id=moved(at, "z", 1 if right else -1, NZ),
            device_id_type=MESH,
        )

    def send(right, s, sub, add):
        d = (4 - s) if right else (4 + s)
        q = slot_of[d]
        need(q)
        if add:
            copy(right, s - 1, sub).wait_recv()

        @pl.loop(sub * SUB, (sub + 1) * SUB)
        def _(b):
            v = own[q, b].astype(F32) + sib[q, b].astype(F32)
            if add:
                v = v + (in_r if right else in_l)[s - 1, b].astype(F32)
            (out_r if right else out_l)[s, b] = v.astype(BF16)

        c = copy(right, s, sub)
        c.start()
        sent.append(c)

    for sub in (0, 1):
        send(True, 0, sub, False)
        send(False, 0, sub + 2, False)
    for sub in (0, 1):
        send(True, 1, sub + 2, False)
        send(False, 1, sub, False)
    for sub in (0, 1):
        send(True, 1, sub, True)
        send(False, 1, sub + 2, True)
    for s in (2, 3):
        for sub in (2, 3, 0, 1):
            send(True, s, sub, True)
            send(False, s, (sub + 2) % 4, True)
    q = slot_of[0]
    need(q)
    gram_ref[...] = jnp.zeros((T, T), F32)
    for sub in (2, 3, 0, 1):
        copy(True, 3, sub).wait_recv()
        copy(False, 3, sub).wait_recv()

        @pl.loop(sub * SUB, (sub + 1) * SUB)
        def _(b):
            v = own[q, b].astype(F32) + sib[q, b].astype(F32)
            v = v + in_r[3, b].astype(F32) + in_l[3, b].astype(F32)
            w = idf_ref[pl.ds(b, 1), :]
            v = v * w
            st_ref[b] = v
            wt_ref[b] = (v * w).astype(BF16)
            gram_ref[...] += lax.dot_general(v, v, NT, precision=HIGH, preferred_element_type=F32)

    for c in theirs:
        c.wait_send()
    for c in sent:
        c.wait_send()


def reduce_sketch(parts, idf):
    dma = pltpu.SemaphoreType.DMA
    return pl.pallas_call(
        reduce_kernel,
        out_shape=(
            jax.ShapeDtypeStruct((16, T, T), F32),
            jax.ShapeDtypeStruct((16, T, T), BF16),
            jax.ShapeDtypeStruct((T, T), F32),
        ),
        in_specs=[ANY, VMEM],
        out_specs=(VMEM, VMEM, VMEM),
        scratch_shapes=[
            pltpu.VMEM((8, 16, T, T), BF16),
            pltpu.VMEM((8, 16, T, T), BF16),
            *[pltpu.VMEM((4, 16, T, T), BF16)] * 4,
            dma((8,)), dma((8,)), dma((8,)),
            *[dma((4, 4))] * 4,
        ],
        compiler_params=params(40, 2),
        name="sketch_reduce",
    )(parts.reshape(16, 16, T, T), idf.reshape(16, T))


def gram_kernel(
    g_ref, out_ref, half, from_sib, over_z, piece, over_xy, total, whole,
    a_send, a_recv, z_send, z_recv, p_send, p_recv, b_send, b_recv, s_send, s_recv,
):
    at = place()
    z, c, x, y = (at[a] for a in AXES)
    sibling = (z, 1 - c, x, y)
    z_peers = [moved(at, "z", d, NZ) for d in range(1, NZ)]
    xy_peers = [
        (z, c, lax.rem(x + i, 4), lax.rem(y + j, 4)) for i in range(4) for j in range(4) if i or j
    ]
    greet([sibling, *z_peers, *xy_peers])

    def put(src, dst, ss, rs, device):
        return pltpu.make_async_remote_copy(
            src_ref=src, dst_ref=dst, send_sem=ss, recv_sem=rs, device_id=device, device_id_type=MESH
        )

    def rows(i, n):
        return pl.ds(pl.multiple_of(i * n, n), n)

    one = put(g_ref.at[rows(1 - c, 64)], from_sib, a_send, a_recv, sibling)
    one.start()
    one.wait()
    half[...] = g_ref[rows(c, 64), :] + from_sib[...]
    copies = []
    for d, peer in enumerate(z_peers):
        cp = put(half.at[rows(peer[0], 8)], over_z.at[z], z_send.at[d], z_recv.at[d], peer)
        cp.start()
        copies.append(cp)
    over_z[z] = half[rows(z, 8), :]
    for cp in copies:
        cp.wait()
    piece[...] = functools.reduce(lambda u, v: u + v, [over_z[i] for i in range(NZ)])
    copies = []
    me = x * 4 + y
    for d, peer in enumerate(xy_peers):
        cp = put(piece, over_xy.at[me], p_send.at[d], p_recv.at[d], peer)
        cp.start()
        copies.append(cp)
    over_xy[me] = piece[...]
    for cp in copies:
        cp.wait()
    total[rows(z, 8), :] = functools.reduce(lambda u, v: u + v, [over_xy[i] for i in range(16)])
    copies = []
    for d, peer in enumerate(z_peers):
        cp = put(total.at[rows(z, 8)], total.at[rows(z, 8)], b_send.at[d], b_recv.at[d], peer)
        cp.start()
        copies.append(cp)
    for cp in copies:
        cp.wait()
    one = put(total, whole.at[rows(c, 64)], s_send, s_recv, sibling)
    one.start()
    whole[rows(c, 64), :] = total[...]
    one.wait()
    out_ref[...] = whole[...]


def sum_gram(gram):
    dma = pltpu.SemaphoreType.DMA
    return pl.pallas_call(
        gram_kernel,
        out_shape=jax.ShapeDtypeStruct((T, T), F32),
        in_specs=[VMEM],
        out_specs=VMEM,
        scratch_shapes=[
            pltpu.VMEM((64, T), F32),
            pltpu.VMEM((64, T), F32),
            pltpu.VMEM((8, 8, T), F32),
            pltpu.VMEM((8, T), F32),
            pltpu.VMEM((16, 8, T), F32),
            pltpu.VMEM((64, T), F32),
            pltpu.VMEM((T, T), F32),
            dma, dma, dma((7,)), dma((7,)), dma((15,)), dma((15,)), dma((7,)), dma((7,)), dma, dma,
        ],
        compiler_params=params(16, 3),
        cost_estimate=pl.CostEstimate(flops=20_000_000_000, bytes_accessed=131072, transcendentals=0),
        name="gram_sum",
    )(gram)


def basis_kernel(terms, gram_ref, st_ref, q_ref, linv_ref, work, pivots):
    work[:, :T] = gram_ref[...] * (1.0 / terms)
    row = lax.broadcasted_iota(jnp.int32, (T, T), 0)
    lane = lax.broadcasted_iota(jnp.int32, (T, T), 1)
    work[:, T:] = (row == lane).astype(F32)
    pivots[...] = jnp.zeros((T, T), F32)

    @pl.loop(0, T)
    def _(j):
        line = work[pl.ds(j, 1), :]
        pivot = jnp.sum(jnp.where(lane[:1] == j, line[:, :T], 0.0), axis=1, keepdims=True)
        scaled = line / pivot
        column = jnp.sum(jnp.where(lane == j, work[:, :T], 0.0), axis=1, keepdims=True)
        column = jnp.where(row[:, :1] > j, column, 0.0)
        work[...] = work[...] - column * scaled
        pivots[pl.ds(j, 1), :] = jnp.broadcast_to(pivot, (1, T))

    linv = work[:, T:] * lax.rsqrt(pivots[...])
    linv_ref[...] = linv

    @pl.loop(0, 16)
    def _(b):
        q_ref[pl.ds(b * T, T), :] = lax.dot_general(
            st_ref[b], linv, (((0,), (1,)), ((), ())), precision=HIGH, preferred_element_type=F32
        )


def basis(gram, st, terms):
    return pl.pallas_call(
        functools.partial(basis_kernel, terms),
        out_shape=(jax.ShapeDtypeStruct((16 * T, T), F32), jax.ShapeDtypeStruct((T, T), F32)),
        in_specs=[VMEM, VMEM],
        out_specs=(VMEM, VMEM),
        scratch_shapes=[pltpu.VMEM((T, 2 * T), F32), pltpu.VMEM((T, T), F32)],
        compiler_params=params(16),
        cost_estimate=pl.CostEstimate(flops=20_000_000_000, bytes_accessed=2 * MIB, transcendentals=0),
        name="basis",
    )(gram, st)


def project_kernel(col, group, slot, live, tiles_ref, w_ref, acc):
    step = pl.program_id(0)

    @pl.when(step == 0)
    def _():
        @pl.loop(0, 64)
        def _(i):
            acc[i] = jnp.zeros((T, T), F32)

    @pl.loop(0, STEP, unroll=2)
    def _(i):
        r = step * STEP + i
        tile_row = jnp.concatenate([tiles_ref[i, j] for j in range(5)], axis=1)
        w = w_ref[group[r] * 16 + slot[r]]
        w = jnp.where(r < live[0], w, jnp.zeros_like(w))
        part = jnp.dot(w, tile_row, preferred_element_type=F32)
        for j in range(5):
            c = col[r, j]
            dev, b = c // 4, c % 4
            flow = b // 2
            u, v = dev // 4, dev % 4
            t = jnp.where(flow == 0, u * 4 + v, v * 4 + u)
            acc[flow * 32 + t * 2 + b % 2] += part[:, j * T : (j + 1) * T]


def project(tiles, tile_col, strip_group, strip_slot, live_count, weighted):
    strips = tiles.shape[0]
    return pl.pallas_call(
        project_kernel,
        out_shape=jax.ShapeDtypeStruct((64, T, T), F32),
        grid=(strips // STEP,),
        in_specs=[
            SMEM,
            SMEM,
            SMEM,
            SMEM,
            pl.BlockSpec((STEP, 5, T, T), lambda i: (i, 0, 0, 0)),
            pl.BlockSpec((256, T, T), lambda i: (0, 0, 0)),
        ],
        out_specs=pl.BlockSpec((64, T, T), lambda i: (0, 0, 0)),
        compiler_params=params(48),
        name="project",
    )(tile_col, strip_group, strip_slot, live_count, tiles, weighted)


def ring_sum(at, axis, own, out_refs, in_refs, send, recv, size):
    here = at[axis]
    dtype = out_refs[0].dtype
    low, high = pl.ds(0, size), pl.ds(size, size)
    r0, r1, l0, l1 = range(4)
    sent = []

    def copy(k, src, dst, right):
        return pltpu.make_async_remote_copy(
            src_ref=src,
            dst_ref=dst,
            send_sem=send.at[k],
            recv_sem=recv.at[k],
            device_id=moved(at, axis, 1 if right else -1, 4),
            device_id_type=MESH,
        )

    def fill(k, offset, target, extra=None):
        out = out_refs[k]
        base = 0 if k in (r0, l0) else offset

        @pl.loop(0, size)
        def _(b):
            v = own[target, b + offset]
            if extra is not None:
                v = v + extra[b].astype(F32)
            out[base + b] = v.astype(dtype)

    far = lax.rem(here + 2, 4)
    right, left = lax.rem(here + 1, 4), lax.rem(here + 3, 4)
    c_r0 = copy(0, out_refs[r0], in_refs[r0], True)
    c_l0 = copy(1, out_refs[l0], in_refs[l0], False)
    c_r1q = copy(2, out_refs[r1].at[high], in_refs[r1].at[high], True)
    c_l1p = copy(3, out_refs[l1].at[low], in_refs[l1].at[low], False)
    c_r1p = copy(4, out_refs[r1].at[low], in_refs[r1].at[low], True)
    c_l1q = copy(5, out_refs[l1].at[high], in_refs[l1].at[high], False)
    fill(r0, 0, far)
    c_r0.start()
    fill(l0, size, far)
    c_l0.start()
    yield
    fill(r1, size, right)
    c_r1q.start()
    fill(l1, 0, left)
    c_l1p.start()
    yield
    c_r0.wait_recv()
    fill(r1, 0, right, in_refs[r0])
    c_r1p.start()
    c_l0.wait_recv()
    fill(l1, size, left, in_refs[l0])
    c_l1q.start()
    yield
    for c in (c_r1q, c_l1p, c_r1p, c_l1q):
        c.wait_recv()
    yield
    for c in (c_r0, c_l0, c_r1q, c_l1p, c_r1p, c_l1q):
        c.wait_send()
    yield


def docs_kernel(part_ref, linv_ref, out_ref, *scratch):
    at = place()
    bufs1 = [scratch[0:8], scratch[8:16]]
    bufs2 = [scratch[16:24], scratch[24:32]]
    sums, final, send, recv = scratch[32:]
    greet([moved(at, "x", 1, 4), moved(at, "x", -1, 4), moved(at, "y", 1, 4), moved(at, "y", -1, 4)])
    axes = ("x", "y")
    runs = [
        ring_sum(
            at, axes[f], part_ref.at[f], bufs1[f][:4], bufs1[f][4:], send.at[f], recv.at[f], 4
        )
        for f in range(2)
    ]
    for _ in range(4):
        for run in runs:
            next(run)
    for f in range(2):
        in_r, in_l = bufs1[f][5], bufs1[f][7]
        here = at[axes[f]]

        @pl.loop(0, 8)
        def _(b):
            v = part_ref[f, here, b] + in_r[b].astype(F32) + in_l[b].astype(F32)
            sums[f, b // 2, b % 2] = v

    later = [
        ring_sum(
            at, axes[1 - f], sums.at[f], bufs2[f][:4], bufs2[f][4:], send.at[2 + f], recv.at[2 + f], 1
        )
        for f in range(2)
    ]
    for _ in range(4):
        for run in later:
            next(run)
    for f in range(2):
        in_r, in_l = bufs2[f][5], bufs2[f][7]
        here = at[axes[1 - f]]
        for b in range(2):
            final[2 * f + b] = sums[f, here, b] + in_r[b] + in_l[b]
    for b in range(4):
        out_ref[:, b * T : (b + 1) * T] = jnp.dot(
            linv_ref[...], final[b], precision=HIGH, preferred_element_type=F32
        ).astype(BF16)
    for run in (*runs, *later):
        next(run)


def sum_docs(parts, linv):
    dma = pltpu.SemaphoreType.DMA

    def bufs(size, dtype):
        return [pltpu.VMEM((n * size, T, T), dtype) for n in (1, 2, 1, 2)] * 2

    return pl.pallas_call(
        docs_kernel,
        out_shape=jax.ShapeDtypeStruct((T, 4 * T), BF16),
        in_specs=[VMEM, VMEM],
        out_specs=VMEM,
        scratch_shapes=[
            *bufs(4, BF16),
            *bufs(4, BF16),
            *bufs(1, F32),
            *bufs(1, F32),
            pltpu.VMEM((2, 4, 2, T, T), F32),
            pltpu.VMEM((4, T, T), F32),
            dma((4, 6)),
            dma((4, 6)),
        ],
        compiler_params=params(24, 4),
        name="docs_sum",
    )(parts.reshape(2, 4, 8, T, T), linv)


def on_device(tiles, tile_col, strip_group, strip_slot, live_count, omega, idf):
    terms = idf.shape[0] * 256
    omega_all = gather_omega(omega).reshape(64, T, T)
    where = (tile_col, strip_group, strip_slot, live_count)
    parts = sketch_parts(tiles, *where, omega_all)
    st, wt, gram = reduce_sketch(parts, idf)
    weighted = lax.all_gather(wt, ("z", "c"), axis=0, tiled=True)
    gram = sum_gram(gram)
    q_basis, linv = basis(gram, st, terms)
    doc_parts = project(tiles, *where, weighted)
    doc_factor = sum_docs(doc_parts, linv)
    return q_basis, doc_factor


def solution(mesh):
    torus = Mesh(mesh.devices.reshape(8, 2, 4, 4), AXES)
    in_specs = (
        P(AXES, None, None, None),
        P(AXES, None),
        P(AXES),
        P(AXES),
        P(AXES),
        P(AXES, None),
        P(AXES),
    )
    out_specs = (P(AXES, None), P(None, AXES))
    return jax.shard_map(
        on_device, mesh=torus, in_specs=in_specs, out_specs=out_specs, check_vma=False
    )
```

```python
import functools

import jax
import jax.numpy as jnp
from jax import lax
from jax.experimental import pallas as pl
from jax.experimental.pallas import tpu as pltpu
from jax.sharding import Mesh
from jax.sharding import PartitionSpec as P

AXES = ("z", "c", "x", "y")
MESH = pl.DeviceIdType.MESH
BF16 = jnp.bfloat16
F32 = jnp.float32
T = 128
NZ = 8
HIGH = lax.Precision.HIGHEST
NT = (((1,), (1,)), ((), ()))
ANY = pl.BlockSpec(memory_space=pl.ANY)
VMEM = pl.BlockSpec(memory_space=pltpu.VMEM)
SMEM = pl.BlockSpec(memory_space=pltpu.SMEM)
MIB = 1 << 20


def place():
    return {a: lax.axis_index(a) for a in AXES}


def moved(at, axis, step, size):
    there = dict(at)
    there[axis] = lax.rem(at[axis] + (step + size), size)
    return tuple(there[a] for a in AXES)


def greet(devices):
    barrier = pltpu.get_barrier_semaphore()
    for device in devices:
        pl.semaphore_signal(barrier, inc=1, device_id=device, device_id_type=MESH)
    pl.semaphore_wait(barrier, len(devices))


def params(mib, cid=None):
    if cid is None:
        return pltpu.CompilerParams(vmem_limit_bytes=mib * MIB)
    return pltpu.CompilerParams(
        vmem_limit_bytes=mib * MIB, collective_id=cid, has_side_effects=True
    )


STEP = 8
PER = 6
NONE = 6


def lists_kernel(group, slot, live, strip, before, last, count):
    @pl.loop(0, 16)
    def _(o):
        count[o] = 0

    @pl.loop(0, 256, unroll=8)
    def _(k):
        last[k] = NONE

    @pl.loop(0, 16 * PER, unroll=8)
    def _(k):
        strip[k] = 0
        before[k] = NONE

    @pl.loop(0, live[0])
    def _(r):
        o = group[r]
        n = count[o]
        at = o * 16 + slot[r]
        strip[o * PER + n] = r
        before[o * PER + n] = last[at]
        last[at] = n
        count[o] = n + 1


def strip_lists(strip_group, strip_slot, live_count):
    ints = jnp.int32
    return pl.pallas_call(
        lists_kernel,
        out_shape=(
            jax.ShapeDtypeStruct((16 * PER,), ints),
            jax.ShapeDtypeStruct((16 * PER,), ints),
            jax.ShapeDtypeStruct((256,), ints),
        ),
        in_specs=[SMEM, SMEM, SMEM],
        out_specs=(SMEM, SMEM, SMEM),
        scratch_shapes=[pltpu.SMEM((16,), ints)],
        name="strip_lists",
    )(strip_group, strip_slot, live_count)


ORDER = (4, 3, 5, 2, 6, 1, 7, 0)
SUB = 4
SUBW = 2
NW = 8


def gather_omega(at, omega_ref, om, send, recv):
    def index(axis, step):
        there = moved(at, axis, step, 4)
        return there[2] * 4 + there[3]

    def index2(first, step1, second, step2):
        there = dict(at)
        there[first] = lax.rem(at[first] + (step1 + 4), 4)
        there[second] = lax.rem(at[second] + (step2 + 4), 4)
        return there["x"] * 4 + there["y"]

    me = at["x"] * 4 + at["y"]

    def copy(i, k, axis, step, dev, lo, n):
        part = om.at[pl.ds(dev * 4 + lo, n)]
        return pltpu.make_async_remote_copy(
            src_ref=part,
            dst_ref=part,
            send_sem=send.at[i, k],
            recv_sem=recv.at[i, k],
            device_id=moved(at, axis, step, 4),
            device_id_type=MESH,
        )

    sent = []

    def go(*args):
        c = copy(*args)
        c.start()
        sent.append(c)

    def begin(i, axis, dev, h):
        go(i, 0, axis, 1, dev, 2 * h, 2)
        go(i, 1, axis, -1, dev, 2 * h, 2)

    def got(i, k, axis, dev, lo, n):
        copy(i, k, axis, 1, dev, lo, n).wait_recv()

    turns = ((0, "x", "y"), (1, "y", "x"))
    for h, a, b in turns:
        begin(5 * h, a, me, h)
    for h, a, b in turns:
        begin(5 * h + 1, b, me, h)
    for h, a, b in turns:
        i = 5 * h
        got(i, 0, a, index(a, -1), 2 * h, 2)
        go(i, 2, a, 1, index(a, -1), 2 * h, 1)
        begin(5 * h + 2, b, index(a, -1), h)
        got(i, 1, a, index(a, 1), 2 * h, 2)
        go(i, 3, a, -1, index(a, 1), 2 * h + 1, 1)
        begin(5 * h + 3, b, index(a, 1), h)
    for h, a, b in turns:
        i = 5 * h
        got(i, 2, a, index(a, 2), 2 * h, 1)
        got(i, 3, a, index(a, 2), 2 * h + 1, 1)
        begin(5 * h + 4, b, index(a, 2), h)
    steps = ((1, 0), (2, -1), (3, 1), (4, 2))
    for k, d in steps:
        for h, a, b in turns:
            i = 5 * h + k
            got(i, 0, b, index2(a, d, b, -1), 2 * h, 2)
            go(i, 2, b, 1, index2(a, d, b, -1), 2 * h, 1)
            got(i, 1, b, index2(a, d, b, 1), 2 * h, 2)
            go(i, 3, b, -1, index2(a, d, b, 1), 2 * h + 1, 1)
    for k, d in steps:
        for h, a, b in turns:
            i = 5 * h + k
            got(i, 2, b, index2(a, d, b, 2), 2 * h, 1)
            got(i, 3, b, index2(a, d, b, 2), 2 * h + 1, 1)
    return sent


def gram_steps(at, g_ref, whole, half, from_sib, over_z, piece, over_xy, total, sems):
    z, c, x, y = (at[a] for a in AXES)
    sibling = (z, 1 - c, x, y)
    a_send, a_recv, z_send, z_recv, p_send, p_recv, b_send, b_recv, s_send, s_recv = sems

    def put(src, dst, ss, rs, device):
        cp = pltpu.make_async_remote_copy(
            src_ref=src, dst_ref=dst, send_sem=ss, recv_sem=rs, device_id=device, device_id_type=MESH
        )
        cp.start()
        return cp

    def rows(i, n):
        return pl.ds(pl.multiple_of(i * n, n), n)

    one = put(g_ref.at[rows(1 - c, 64)], from_sib, a_send, a_recv, sibling)
    yield
    one.wait()
    half[...] = g_ref[rows(c, 64), :] + from_sib[...]
    z_peers = [moved(at, "z", d, NZ) for d in range(1, NZ)]
    copies = [
        put(half.at[rows(p[0], 8)], over_z.at[z], z_send.at[d], z_recv.at[d], p)
        for d, p in enumerate(z_peers)
    ]
    over_z[z] = half[rows(z, 8), :]
    yield
    for cp in copies:
        cp.wait()
    piece[...] = functools.reduce(lambda u, v: u + v, [over_z[i] for i in range(NZ)])
    me = x * 4 + y
    copies = [
        put(piece, over_xy.at[me], p_send.at[d], p_recv.at[d], p) for d, p in enumerate(xy_others(at))
    ]
    over_xy[me] = piece[...]
    yield
    for cp in copies:
        cp.wait()
    total[rows(z, 8), :] = functools.reduce(lambda u, v: u + v, [over_xy[i] for i in range(16)])
    copies = [
        put(total.at[rows(z, 8)], total.at[rows(z, 8)], b_send.at[d], b_recv.at[d], p)
        for d, p in enumerate(z_peers)
    ]
    yield
    for cp in copies:
        cp.wait()
    one = put(total, whole.at[rows(c, 64)], s_send, s_recv, sibling)
    whole[rows(c, 64), :] = total[...]
    yield
    one.wait()
    yield


def xy_others(at):
    z, c, x, y = (at[a] for a in AXES)
    return [(z, c, lax.rem(x + i, 4), lax.rem(y + j, 4)) for i in range(4) for j in range(4) if i or j]


def eliminate(terms, gram, linv_ref, work, pivots):
    work[:, :T] = gram[...] * (1.0 / terms)
    row = lax.broadcasted_iota(jnp.int32, (T, T), 0)
    lane = lax.broadcasted_iota(jnp.int32, (T, T), 1)
    work[:, T:] = (row == lane).astype(F32)
    pivots[...] = jnp.zeros((T, T), F32)
    for first in range(0, T, 16):

        @pl.loop(first, first + 16)
        def _(j):
            line = work[pl.ds(j, 1), :]
            pivot = jnp.sum(jnp.where(lane[:1] == j, line[:, :T], 0.0), axis=1, keepdims=True)
            scaled = line / pivot
            column = jnp.sum(jnp.where(lane == j, work[:, :T], 0.0), axis=1, keepdims=True)
            column = jnp.where(row[:, :1] > j, column, 0.0)
            work[...] = work[...] - column * scaled
            pivots[pl.ds(j, 1), :] = jnp.broadcast_to(pivot, (1, T))

        yield
    linv_ref[...] = work[:, T:] * lax.rsqrt(pivots[...])
    yield


def front_kernel(
    terms, strip, before, last, col, omega_ref, idf_ref, tiles_ref, w_ref, st_ref, linv_ref,
    tiles, om, raw, chain, own, out_sib, sib, out_r, out_l, in_r, in_l, wt, gram,
    whole, half, from_sib, over_z, piece, over_xy, total, work, pivots,
    load_sem, om_send, om_recv, sib_send, sib_recv, r_send, r_recv, l_send, l_recv,
    own_sem, wr_send, wr_recv, wl_send, wl_recv, ws_send, ws_recv, *gram_sems,
):
    at = place()
    load = pltpu.make_async_copy(tiles_ref, tiles, load_sem)
    load.start()
    sibling = (at["z"], 1 - at["c"], at["x"], at["y"])
    me = at["x"] * 4 + at["y"]
    for b in range(4):
        om[me * 4 + b] = omega_ref[b * T : (b + 1) * T, :].T
    greet([sibling, *[moved(at, "z", d, NZ) for d in range(1, NZ)], *xy_others(at)])
    sent = gather_omega(at, omega_ref, om, om_send, om_recv)

    @pl.loop(0, 2 * (PER + 1))
    def _(k):
        chain[k] = jnp.zeros((T, T), F32)

    load.wait()
    slot_of = {d: q for q, d in enumerate(ORDER)}

    def sketch(d):
        q = slot_of[d]
        z = lax.rem(at["z"] + d, NZ)
        for k, target in ((0, out_sib), (1, own)):
            o = 2 * z + (1 - at["c"] if k == 0 else at["c"])
            base = k * (PER + 1)

            @pl.loop(0, PER, unroll=3)
            def _(n):
                i = strip[o * PER + n]
                tile_row = jnp.concatenate([tiles[i, j] for j in range(5)], axis=1)
                m = jnp.concatenate([om[col[i, j]] for j in range(5)], axis=1)
                raw[k * PER + n] = lax.dot_general(m, tile_row, NT, preferred_element_type=F32)

            @pl.loop(0, PER)
            def _(n):
                chain[base + n] = raw[k * PER + n] + chain[base + before[o * PER + n]]

            @pl.loop(0, 16, unroll=2)
            def _(b):
                target[q, b] = chain[base + last[o * 16 + b]].astype(BF16)

            if k == 0:
                c = pltpu.make_async_remote_copy(
                    src_ref=out_sib.at[q],
                    dst_ref=sib.at[q],
                    send_sem=sib_send.at[q],
                    recv_sem=sib_recv.at[q],
                    device_id=sibling,
                    device_id_type=MESH,
                )
                c.start()
        sent.append(c)
        theirs[q] = c

    theirs = {}
    ready = set()

    def need(q):
        if q not in ready:
            ready.add(q)
            theirs[q].wait_recv()

    def copy(right, s, sub):
        rows = pl.ds(sub * SUB, SUB)
        return pltpu.make_async_remote_copy(
            src_ref=(out_r if right else out_l).at[s, rows],
            dst_ref=(in_r if right else in_l).at[s, rows],
            send_sem=(r_send if right else l_send).at[s, sub],
            recv_sem=(r_recv if right else l_recv).at[s, sub],
            device_id=moved(at, "z", 1 if right else -1, NZ),
            device_id_type=MESH,
        )

    def send(right, s, sub, add):
        d = (4 - s) if right else (4 + s)
        q = slot_of[d]
        need(q)
        if add:
            copy(right, s - 1, sub).wait_recv()

        @pl.loop(sub * SUB, (sub + 1) * SUB)
        def _(b):
            v = own[q, b].astype(F32) + sib[q, b].astype(F32)
            if add:
                v = v + (in_r if right else in_l)[s - 1, b].astype(F32)
            (out_r if right else out_l)[s, b] = v.astype(BF16)

        c = copy(right, s, sub)
        c.start()
        sent.append(c)

    sketch(4)
    for sub in (0, 1):
        send(True, 0, sub, False)
        send(False, 0, sub + 2, False)
    sketch(3)
    sketch(5)
    for sub in (0, 1):
        send(True, 1, sub + 2, False)
        send(False, 1, sub, False)
    for sub in (0, 1):
        send(True, 1, sub, True)
        send(False, 1, sub + 2, True)
    sketch(2)
    sketch(6)
    for s in (2, 3):
        for sub in (2, 3, 0, 1):
            send(True, s, sub, True)
            send(False, s, (sub + 2) % 4, True)
        if s == 2:
            sketch(1)
            sketch(7)
    sketch(0)

    mine = 2 * at["z"] + at["c"]

    def wcopy(right, hop, sub):
        owner = 2 * lax.rem(at["z"] + ((1 - hop) if right else (hop - 1)) + NZ, NZ) + at["c"]
        rows = pl.ds(sub * SUBW, SUBW)
        return pltpu.make_async_remote_copy(
            src_ref=wt.at[rows] if hop == 1 else w_ref.at[owner, rows],
            dst_ref=w_ref.at[owner, rows],
            send_sem=(wr_send if right else wl_send).at[hop - 1, sub],
            recv_sem=(wr_recv if right else wl_recv).at[hop - 1, sub],
            device_id=moved(at, "z", 1 if right else -1, NZ),
            device_id_type=MESH,
        )

    def wgo(right, hop, sub):
        c = wcopy(right, hop, sub)
        c.start()
        sent.append(c)

    def to_sibling(d):
        owner = 2 * lax.rem(at["z"] + d, NZ) + at["c"]
        c = pltpu.make_async_remote_copy(
            src_ref=wt if d == 0 else w_ref.at[owner],
            dst_ref=w_ref.at[owner],
            send_sem=ws_send.at[d],
            recv_sem=ws_recv.at[d],
            device_id=sibling,
            device_id_type=MESH,
        )
        c.start()
        passed.append(c)

    passed = []
    q = slot_of[0]
    need(q)
    gram[...] = jnp.zeros((T, T), F32)
    for sub in (2, 3, 0, 1):
        copy(True, 3, sub).wait_recv()
        copy(False, 3, sub).wait_recv()

        @pl.loop(sub * SUB, (sub + 1) * SUB)
        def _(b):
            v = own[q, b].astype(F32) + sib[q, b].astype(F32)
            v = v + in_r[3, b].astype(F32) + in_l[3, b].astype(F32)
            w = idf_ref[pl.ds(b, 1), :]
            v = v * w
            st_ref[b] = v
            wt[b] = (v * w).astype(BF16)

        for k in range(SUB // SUBW):
            wgo(True, 1, sub * (SUB // SUBW) + k)
            wgo(False, 1, sub * (SUB // SUBW) + k)
    to_sibling(0)
    keep = pltpu.make_async_copy(wt, w_ref.at[mine], own_sem)
    keep.start()

    @pl.loop(0, 16)
    def _(b):
        v = st_ref[b]
        gram[...] += lax.dot_general(v, v, NT, precision=HIGH, preferred_element_type=F32)

    def side():
        yield from gram_steps(
            at, gram, whole, half, from_sib, over_z, piece, over_xy, total, gram_sems
        )
        yield from eliminate(terms, whole, linv_ref, work, pivots)

    aside = side()
    next(aside)
    order = (4, 5, 6, 7, 0, 1, 2, 3)
    for hop in (2, 3, 4):
        for n, sub in enumerate(order):
            wcopy(True, hop - 1, sub).wait_recv()
            if hop < 4 or sub < NW // 2:
                wgo(True, hop, sub)
            wcopy(False, hop - 1, sub).wait_recv()
            if hop < 4 or sub >= NW // 2:
                wgo(False, hop, sub)
            if n % 2 == 1:
                next(aside, None)
        to_sibling(hop - 1)
        to_sibling(NZ - (hop - 1))
    for _ in aside:
        pass
    for sub in range(NW // 2):
        wcopy(True, 4, sub).wait_recv()
        wcopy(False, 4, sub + NW // 2).wait_recv()
    to_sibling(4)
    keep.wait()
    for c in passed:
        c.wait()
    for c in sent:
        c.wait_send()


def front(lists, tile_col, tiles, omega, idf, terms):
    dma = pltpu.SemaphoreType.DMA
    v = pltpu.VMEM
    return pl.pallas_call(
        functools.partial(front_kernel, terms),
        out_shape=(
            jax.ShapeDtypeStruct((16, 16, T, T), BF16),
            jax.ShapeDtypeStruct((16, T, T), F32),
            jax.ShapeDtypeStruct((T, T), F32),
        ),
        in_specs=[SMEM, SMEM, SMEM, SMEM, VMEM, VMEM, ANY],
        out_specs=(ANY, VMEM, VMEM),
        scratch_shapes=[
            v(tiles.shape, BF16),
            v((64, T, T), BF16),
            v((2 * PER, T, T), F32),
            v((2 * (PER + 1), T, T), F32),
            *[v((8, 16, T, T), BF16)] * 3,
            *[v((4, 16, T, T), BF16)] * 4,
            v((16, T, T), BF16),
            v((T, T), F32),
            v((T, T), F32),
            v((64, T), F32),
            v((64, T), F32),
            v((8, 8, T), F32),
            v((8, T), F32),
            v((16, 8, T), F32),
            v((64, T), F32),
            v((T, 2 * T), F32),
            v((T, T), F32),
            dma,
            dma((10, 4)), dma((10, 4)),
            dma((8,)), dma((8,)),
            *[dma((4, 4))] * 4,
            dma,
            *[dma((4, NW))] * 4,
            dma((8,)), dma((8,)),
            dma, dma, dma((7,)), dma((7,)), dma((15,)), dma((15,)), dma((7,)), dma((7,)), dma, dma,
        ],
        compiler_params=params(54, 1),
        name="front",
    )(*lists, tile_col, omega, idf.reshape(16, T), tiles)


def project_kernel(col, group, slot, live, tiles_ref, w_ref, st_ref, linv_ref, acc, q_ref):
    step = pl.program_id(0)

    @pl.when(step == 0)
    def _():
        @pl.loop(0, 64)
        def _(i):
            acc[i] = jnp.zeros((T, T), F32)

    @pl.loop(0, 2)
    def _(i):
        b = jnp.minimum(2 * step + i, 15)
        q_ref[pl.ds(b * T, T), :] = lax.dot_general(
            st_ref[b], linv_ref[...], (((0,), (1,)), ((), ())), precision=HIGH, preferred_element_type=F32
        )

    @pl.loop(0, STEP, unroll=2)
    def _(i):
        r = step * STEP + i
        tile_row = jnp.concatenate([tiles_ref[i, j] for j in range(5)], axis=1)
        w = w_ref[group[r] * 16 + slot[r]]
        w = jnp.where(r < live[0], w, jnp.zeros_like(w))
        part = jnp.dot(w, tile_row, preferred_element_type=F32)
        for j in range(5):
            c = col[r, j]
            dev, b = c // 4, c % 4
            flow = b // 2
            u, v = dev // 4, dev % 4
            t = jnp.where(flow == 0, u * 4 + v, v * 4 + u)
            acc[flow * 32 + t * 2 + b % 2] += part[:, j * T : (j + 1) * T]


def project(tiles, tile_col, strip_group, strip_slot, live_count, weighted, st, linv):
    strips = tiles.shape[0]
    return pl.pallas_call(
        project_kernel,
        out_shape=(
            jax.ShapeDtypeStruct((64, T, T), F32),
            jax.ShapeDtypeStruct((16 * T, T), F32),
        ),
        grid=(strips // STEP,),
        in_specs=[
            SMEM,
            SMEM,
            SMEM,
            SMEM,
            pl.BlockSpec((STEP, 5, T, T), lambda i: (i, 0, 0, 0)),
            pl.BlockSpec((256, T, T), lambda i: (0, 0, 0)),
            pl.BlockSpec((16, T, T), lambda i: (0, 0, 0)),
            pl.BlockSpec((T, T), lambda i: (0, 0)),
        ],
        out_specs=(
            pl.BlockSpec((64, T, T), lambda i: (0, 0, 0)),
            pl.BlockSpec((16 * T, T), lambda i: (0, 0)),
        ),
        compiler_params=params(48),
        name="project",
    )(tile_col, strip_group, strip_slot, live_count, tiles, weighted.reshape(256, T, T), st, linv)


def ring_sum(at, axis, own, out_refs, in_refs, send, recv, size):
    here = at[axis]
    dtype = out_refs[0].dtype
    low, high = pl.ds(0, size), pl.ds(size, size)
    r0, r1, l0, l1 = range(4)
    sent = []

    def copy(k, src, dst, right):
        return pltpu.make_async_remote_copy(
            src_ref=src,
            dst_ref=dst,
            send_sem=send.at[k],
            recv_sem=recv.at[k],
            device_id=moved(at, axis, 1 if right else -1, 4),
            device_id_type=MESH,
        )

    def fill(k, offset, target, extra=None):
        out = out_refs[k]
        base = 0 if k in (r0, l0) else offset

        @pl.loop(0, size)
        def _(b):
            v = own[target, b + offset]
            if extra is not None:
                v = v + extra[b].astype(F32)
            out[base + b] = v.astype(dtype)

    far = lax.rem(here + 2, 4)
    right, left = lax.rem(here + 1, 4), lax.rem(here + 3, 4)
    c_r0 = copy(0, out_refs[r0], in_refs[r0], True)
    c_l0 = copy(1, out_refs[l0], in_refs[l0], False)
    c_r1q = copy(2, out_refs[r1].at[high], in_refs[r1].at[high], True)
    c_l1p = copy(3, out_refs[l1].at[low], in_refs[l1].at[low], False)
    c_r1p = copy(4, out_refs[r1].at[low], in_refs[r1].at[low], True)
    c_l1q = copy(5, out_refs[l1].at[high], in_refs[l1].at[high], False)
    fill(r0, 0, far)
    c_r0.start()
    fill(l0, size, far)
    c_l0.start()
    yield
    fill(r1, size, right)
    c_r1q.start()
    fill(l1, 0, left)
    c_l1p.start()
    yield
    c_r0.wait_recv()
    fill(r1, 0, right, in_refs[r0])
    c_r1p.start()
    c_l0.wait_recv()
    fill(l1, size, left, in_refs[l0])
    c_l1q.start()
    yield
    for c in (c_r1q, c_l1p, c_r1p, c_l1q):
        c.wait_recv()
    yield
    for c in (c_r0, c_l0, c_r1q, c_l1p, c_r1p, c_l1q):
        c.wait_send()
    yield


def docs_kernel(part_ref, linv_ref, out_ref, *scratch):
    at = place()
    bufs1 = [scratch[0:8], scratch[8:16]]
    bufs2 = [scratch[16:24], scratch[24:32]]
    sums, final, send, recv = scratch[32:]
    greet([moved(at, "x", 1, 4), moved(at, "x", -1, 4), moved(at, "y", 1, 4), moved(at, "y", -1, 4)])
    axes = ("x", "y")
    runs = [
        ring_sum(
            at, axes[f], part_ref.at[f], bufs1[f][:4], bufs1[f][4:], send.at[f], recv.at[f], 4
        )
        for f in range(2)
    ]
    for _ in range(4):
        for run in runs:
            next(run)
    for f in range(2):
        in_r, in_l = bufs1[f][5], bufs1[f][7]
        here = at[axes[f]]

        @pl.loop(0, 8)
        def _(b):
            v = part_ref[f, here, b] + in_r[b].astype(F32) + in_l[b].astype(F32)
            sums[f, b // 2, b % 2] = v

    later = [
        ring_sum(
            at, axes[1 - f], sums.at[f], bufs2[f][:4], bufs2[f][4:], send.at[2 + f], recv.at[2 + f], 1
        )
        for f in range(2)
    ]
    for _ in range(4):
        for run in later:
            next(run)
    for f in range(2):
        in_r, in_l = bufs2[f][5], bufs2[f][7]
        here = at[axes[1 - f]]
        for b in range(2):
            final[2 * f + b] = sums[f, here, b] + in_r[b] + in_l[b]
    for b in range(4):
        out_ref[:, b * T : (b + 1) * T] = jnp.dot(
            linv_ref[...], final[b], precision=HIGH, preferred_element_type=F32
        ).astype(BF16)
    for run in (*runs, *later):
        next(run)


def sum_docs(parts, linv):
    dma = pltpu.SemaphoreType.DMA

    def bufs(size, dtype):
        return [pltpu.VMEM((n * size, T, T), dtype) for n in (1, 2, 1, 2)] * 2

    return pl.pallas_call(
        docs_kernel,
        out_shape=jax.ShapeDtypeStruct((T, 4 * T), BF16),
        in_specs=[VMEM, VMEM],
        out_specs=VMEM,
        scratch_shapes=[
            *bufs(4, BF16),
            *bufs(4, BF16),
            *bufs(1, F32),
            *bufs(1, F32),
            pltpu.VMEM((2, 4, 2, T, T), F32),
            pltpu.VMEM((4, T, T), F32),
            dma((4, 6)),
            dma((4, 6)),
        ],
        compiler_params=params(24, 4),
        name="docs_sum",
    )(parts.reshape(2, 4, 8, T, T), linv)


def on_device(tiles, tile_col, strip_group, strip_slot, live_count, omega, idf):
    terms = idf.shape[0] * 256
    lists = strip_lists(strip_group, strip_slot, live_count)
    weighted, st, linv = front(lists, tile_col, tiles, omega, idf, terms)
    where = (tile_col, strip_group, strip_slot, live_count)
    doc_parts, q_basis = project(tiles, *where, weighted, st, linv)
    doc_factor = sum_docs(doc_parts, linv)
    return q_basis, doc_factor


def solution(mesh):
    torus = Mesh(mesh.devices.reshape(8, 2, 4, 4), AXES)
    in_specs = (
        P(AXES, None, None, None),
        P(AXES, None),
        P(AXES),
        P(AXES),
        P(AXES),
        P(AXES, None),
        P(AXES),
    )
    out_specs = (P(AXES, None), P(None, AXES))
    return jax.shard_map(
        on_device, mesh=torus, in_specs=in_specs, out_specs=out_specs, check_vma=False
    )
```

```python
import functools

import jax
import jax.numpy as jnp
from jax import lax
from jax.experimental import pallas as pl
from jax.experimental.pallas import tpu as pltpu
from jax.sharding import Mesh
from jax.sharding import PartitionSpec as P

AXES = ("z", "c", "x", "y")
MESH = pl.DeviceIdType.MESH
BF16 = jnp.bfloat16
F32 = jnp.float32
T = 128
NZ = 8
HIGH = lax.Precision.HIGHEST
NT = (((1,), (1,)), ((), ()))
ANY = pl.BlockSpec(memory_space=pl.ANY)
VMEM = pl.BlockSpec(memory_space=pltpu.VMEM)
SMEM = pl.BlockSpec(memory_space=pltpu.SMEM)
MIB = 1 << 20


def place():
    return {a: lax.axis_index(a) for a in AXES}


def moved(at, axis, step, size):
    there = dict(at)
    there[axis] = lax.rem(at[axis] + (step + size), size)
    return tuple(there[a] for a in AXES)


def greet(devices):
    barrier = pltpu.get_barrier_semaphore()
    for device in devices:
        pl.semaphore_signal(barrier, inc=1, device_id=device, device_id_type=MESH)
    pl.semaphore_wait(barrier, len(devices))


def params(mib, cid=None):
    if cid is None:
        return pltpu.CompilerParams(vmem_limit_bytes=mib * MIB)
    return pltpu.CompilerParams(
        vmem_limit_bytes=mib * MIB, collective_id=cid, has_side_effects=True
    )


STEP = 8
PER = 6
NONE = 6


def lists_kernel(group, slot, live, strip, before, last, count):
    @pl.loop(0, 16)
    def _(o):
        count[o] = 0

    @pl.loop(0, 256, unroll=8)
    def _(k):
        last[k] = NONE

    @pl.loop(0, 16 * PER, unroll=8)
    def _(k):
        strip[k] = 0
        before[k] = NONE

    @pl.loop(0, live[0])
    def _(r):
        o = group[r]
        n = count[o]
        at = o * 16 + slot[r]
        strip[o * PER + n] = r
        before[o * PER + n] = last[at]
        last[at] = n
        count[o] = n + 1


def strip_lists(strip_group, strip_slot, live_count):
    ints = jnp.int32
    return pl.pallas_call(
        lists_kernel,
        out_shape=(
            jax.ShapeDtypeStruct((16 * PER,), ints),
            jax.ShapeDtypeStruct((16 * PER,), ints),
            jax.ShapeDtypeStruct((256,), ints),
        ),
        in_specs=[SMEM, SMEM, SMEM],
        out_specs=(SMEM, SMEM, SMEM),
        scratch_shapes=[pltpu.SMEM((16,), ints)],
        name="strip_lists",
    )(strip_group, strip_slot, live_count)


ORDER = (4, 3, 5, 2, 6, 1, 7, 0)
SUB = 4
SUBW = 2
NW = 8


def gather_omega(at, omega_ref, om, send, recv):
    def index(axis, step):
        there = moved(at, axis, step, 4)
        return there[2] * 4 + there[3]

    def index2(first, step1, second, step2):
        there = dict(at)
        there[first] = lax.rem(at[first] + (step1 + 4), 4)
        there[second] = lax.rem(at[second] + (step2 + 4), 4)
        return there["x"] * 4 + there["y"]

    me = at["x"] * 4 + at["y"]

    def copy(i, k, axis, step, dev, lo, n):
        part = om.at[pl.ds(dev * 4 + lo, n)]
        return pltpu.make_async_remote_copy(
            src_ref=part,
            dst_ref=part,
            send_sem=send.at[i, k],
            recv_sem=recv.at[i, k],
            device_id=moved(at, axis, step, 4),
            device_id_type=MESH,
        )

    sent = []

    def go(*args):
        c = copy(*args)
        c.start()
        sent.append(c)

    def begin(i, axis, dev, h):
        go(i, 0, axis, 1, dev, 2 * h, 2)
        go(i, 1, axis, -1, dev, 2 * h, 2)

    def got(i, k, axis, dev, lo, n):
        copy(i, k, axis, 1, dev, lo, n).wait_recv()

    turns = ((0, "x", "y"), (1, "y", "x"))
    for h, a, b in turns:
        begin(5 * h, a, me, h)
    for h, a, b in turns:
        begin(5 * h + 1, b, me, h)
    for h, a, b in turns:
        i = 5 * h
        got(i, 0, a, index(a, -1), 2 * h, 2)
        go(i, 2, a, 1, index(a, -1), 2 * h, 1)
        begin(5 * h + 2, b, index(a, -1), h)
        got(i, 1, a, index(a, 1), 2 * h, 2)
        go(i, 3, a, -1, index(a, 1), 2 * h + 1, 1)
        begin(5 * h + 3, b, index(a, 1), h)
    for h, a, b in turns:
        i = 5 * h
        got(i, 2, a, index(a, 2), 2 * h, 1)
        got(i, 3, a, index(a, 2), 2 * h + 1, 1)
        begin(5 * h + 4, b, index(a, 2), h)
    steps = ((1, 0), (2, -1), (3, 1), (4, 2))
    for k, d in steps:
        for h, a, b in turns:
            i = 5 * h + k
            got(i, 0, b, index2(a, d, b, -1), 2 * h, 2)
            go(i, 2, b, 1, index2(a, d, b, -1), 2 * h, 1)
            got(i, 1, b, index2(a, d, b, 1), 2 * h, 2)
            go(i, 3, b, -1, index2(a, d, b, 1), 2 * h + 1, 1)
    for k, d in steps:
        for h, a, b in turns:
            i = 5 * h + k
            got(i, 2, b, index2(a, d, b, 2), 2 * h, 1)
            got(i, 3, b, index2(a, d, b, 2), 2 * h + 1, 1)
    return sent


def gram_steps(at, g_ref, whole, half, from_sib, over_z, piece, over_xy, total, sems):
    z, c, x, y = (at[a] for a in AXES)
    sibling = (z, 1 - c, x, y)
    a_send, a_recv, z_send, z_recv, p_send, p_recv, b_send, b_recv, s_send, s_recv = sems

    def put(src, dst, ss, rs, device):
        cp = pltpu.make_async_remote_copy(
            src_ref=src, dst_ref=dst, send_sem=ss, recv_sem=rs, device_id=device, device_id_type=MESH
        )
        cp.start()
        return cp

    def rows(i, n):
        return pl.ds(pl.multiple_of(i * n, n), n)

    one = put(g_ref.at[rows(1 - c, 64)], from_sib, a_send, a_recv, sibling)
    yield
    one.wait()
    half[...] = g_ref[rows(c, 64), :] + from_sib[...]
    z_peers = [moved(at, "z", d, NZ) for d in range(1, NZ)]
    copies = [
        put(half.at[rows(p[0], 8)], over_z.at[z], z_send.at[d], z_recv.at[d], p)
        for d, p in enumerate(z_peers)
    ]
    over_z[z] = half[rows(z, 8), :]
    yield
    for cp in copies:
        cp.wait()
    piece[...] = functools.reduce(lambda u, v: u + v, [over_z[i] for i in range(NZ)])
    me = x * 4 + y
    copies = [
        put(piece, over_xy.at[me], p_send.at[d], p_recv.at[d], p) for d, p in enumerate(xy_others(at))
    ]
    over_xy[me] = piece[...]
    yield
    for cp in copies:
        cp.wait()
    total[rows(z, 8), :] = functools.reduce(lambda u, v: u + v, [over_xy[i] for i in range(16)])
    copies = [
        put(total.at[rows(z, 8)], total.at[rows(z, 8)], b_send.at[d], b_recv.at[d], p)
        for d, p in enumerate(z_peers)
    ]
    yield
    for cp in copies:
        cp.wait()
    one = put(total, whole.at[rows(c, 64)], s_send, s_recv, sibling)
    whole[rows(c, 64), :] = total[...]
    yield
    one.wait()
    yield


def xy_others(at):
    z, c, x, y = (at[a] for a in AXES)
    return [(z, c, lax.rem(x + i, 4), lax.rem(y + j, 4)) for i in range(4) for j in range(4) if i or j]


def eliminate(terms, gram, linv_ref, work, pivots):
    work[:, :T] = gram[...] * (1.0 / terms)
    row = lax.broadcasted_iota(jnp.int32, (T, T), 0)
    lane = lax.broadcasted_iota(jnp.int32, (T, T), 1)
    work[:, T:] = (row == lane).astype(F32)
    pivots[...] = jnp.zeros((T, T), F32)
    for first in range(0, T, 16):

        @pl.loop(first, first + 16)
        def _(j):
            line = work[pl.ds(j, 1), :]
            pivot = jnp.sum(jnp.where(lane[:1] == j, line[:, :T], 0.0), axis=1, keepdims=True)
            scaled = line / pivot
            column = jnp.sum(jnp.where(lane == j, work[:, :T], 0.0), axis=1, keepdims=True)
            column = jnp.where(row[:, :1] > j, column, 0.0)
            work[...] = work[...] - column * scaled
            pivots[pl.ds(j, 1), :] = jnp.broadcast_to(pivot, (1, T))

        yield
    linv_ref[...] = work[:, T:] * lax.rsqrt(pivots[...])
    yield


def front_kernel(
    terms, strip, before, last, col, omega_ref, idf_ref, tiles_ref, w_ref, st_ref, linv_ref,
    tiles, om, raw, chain, own, out_sib, sib, out_r, out_l, in_r, in_l, wt, gram,
    whole, half, from_sib, over_z, piece, over_xy, total, work, pivots,
    load_sem, om_send, om_recv, sib_send, sib_recv, r_send, r_recv, l_send, l_recv,
    own_sem, wr_send, wr_recv, wl_send, wl_recv, ws_send, ws_recv, *gram_sems,
):
    at = place()
    load = pltpu.make_async_copy(tiles_ref, tiles, load_sem)
    load.start()
    sibling = (at["z"], 1 - at["c"], at["x"], at["y"])
    me = at["x"] * 4 + at["y"]
    for b in range(4):
        om[me * 4 + b] = omega_ref[b * T : (b + 1) * T, :].T
    near = [moved(at, a, d, 4) for a in ("x", "y") for d in (1, -1)]
    greet([sibling, *near, moved(at, "z", 1, NZ), moved(at, "z", -1, NZ)])
    sent = gather_omega(at, omega_ref, om, om_send, om_recv)

    @pl.loop(0, 2 * (PER + 1))
    def _(k):
        chain[k] = jnp.zeros((T, T), F32)

    load.wait()
    slot_of = {d: q for q, d in enumerate(ORDER)}

    def sketch(d):
        q = slot_of[d]
        z = lax.rem(at["z"] + d, NZ)
        for k, target in ((0, out_sib), (1, own)):
            o = 2 * z + (1 - at["c"] if k == 0 else at["c"])
            base = k * (PER + 1)

            @pl.loop(0, PER, unroll=3)
            def _(n):
                i = strip[o * PER + n]
                tile_row = jnp.concatenate([tiles[i, j] for j in range(5)], axis=1)
                m = jnp.concatenate([om[col[j, i]] for j in range(5)], axis=1)
                raw[k * PER + n] = lax.dot_general(m, tile_row, NT, preferred_element_type=F32)

            @pl.loop(0, PER)
            def _(n):
                chain[base + n] = raw[k * PER + n] + chain[base + before[o * PER + n]]

            @pl.loop(0, 16, unroll=2)
            def _(b):
                target[q, b] = chain[base + last[o * 16 + b]].astype(BF16)

            if k == 0:
                c = pltpu.make_async_remote_copy(
                    src_ref=out_sib.at[q],
                    dst_ref=sib.at[q],
                    send_sem=sib_send.at[q],
                    recv_sem=sib_recv.at[q],
                    device_id=sibling,
                    device_id_type=MESH,
                )
                c.start()
        sent.append(c)
        theirs[q] = c

    theirs = {}
    ready = set()

    def need(q):
        if q not in ready:
            ready.add(q)
            theirs[q].wait_recv()

    def copy(right, s, sub):
        rows = pl.ds(sub * SUB, SUB)
        return pltpu.make_async_remote_copy(
            src_ref=(out_r if right else out_l).at[s, rows],
            dst_ref=(in_r if right else in_l).at[s, rows],
            send_sem=(r_send if right else l_send).at[s, sub],
            recv_sem=(r_recv if right else l_recv).at[s, sub],
            device_id=moved(at, "z", 1 if right else -1, NZ),
            device_id_type=MESH,
        )

    def send(right, s, sub, add):
        d = (4 - s) if right else (4 + s)
        q = slot_of[d]
        need(q)
        if add:
            copy(right, s - 1, sub).wait_recv()

        @pl.loop(sub * SUB, (sub + 1) * SUB)
        def _(b):
            v = own[q, b].astype(F32) + sib[q, b].astype(F32)
            if add:
                v = v + (in_r if right else in_l)[s - 1, b].astype(F32)
            (out_r if right else out_l)[s, b] = v.astype(BF16)

        c = copy(right, s, sub)
        c.start()
        sent.append(c)

    sketch(4)
    for sub in (0, 1):
        send(True, 0, sub, False)
        send(False, 0, sub + 2, False)
    sketch(3)
    sketch(5)
    for sub in (0, 1):
        send(True, 1, sub + 2, False)
        send(False, 1, sub, False)
    for sub in (0, 1):
        send(True, 1, sub, True)
        send(False, 1, sub + 2, True)
    sketch(2)
    sketch(6)
    for s in (2, 3):
        for sub in (2, 3, 0, 1):
            send(True, s, sub, True)
            send(False, s, (sub + 2) % 4, True)
        if s == 2:
            sketch(1)
            sketch(7)
    sketch(0)

    mine = 2 * at["z"] + at["c"]

    def wcopy(right, hop, sub):
        owner = 2 * lax.rem(at["z"] + ((1 - hop) if right else (hop - 1)) + NZ, NZ) + at["c"]
        rows = pl.ds(sub * SUBW, SUBW)
        return pltpu.make_async_remote_copy(
            src_ref=wt.at[rows] if hop == 1 else w_ref.at[owner, rows],
            dst_ref=w_ref.at[owner, rows],
            send_sem=(wr_send if right else wl_send).at[hop - 1, sub],
            recv_sem=(wr_recv if right else wl_recv).at[hop - 1, sub],
            device_id=moved(at, "z", 1 if right else -1, NZ),
            device_id_type=MESH,
        )

    def wgo(right, hop, sub):
        c = wcopy(right, hop, sub)
        c.start()
        sent.append(c)

    def to_sibling(d):
        owner = 2 * lax.rem(at["z"] + d, NZ) + at["c"]
        c = pltpu.make_async_remote_copy(
            src_ref=wt if d == 0 else w_ref.at[owner],
            dst_ref=w_ref.at[owner],
            send_sem=ws_send.at[d],
            recv_sem=ws_recv.at[d],
            device_id=sibling,
            device_id_type=MESH,
        )
        c.start()
        passed.append(c)

    passed = []
    q = slot_of[0]
    need(q)
    gram[...] = jnp.zeros((T, T), F32)
    for sub in (2, 3, 0, 1):
        copy(True, 3, sub).wait_recv()
        copy(False, 3, sub).wait_recv()

        @pl.loop(sub * SUB, (sub + 1) * SUB)
        def _(b):
            v = own[q, b].astype(F32) + sib[q, b].astype(F32)
            v = v + in_r[3, b].astype(F32) + in_l[3, b].astype(F32)
            w = idf_ref[pl.ds(b, 1), :]
            v = v * w
            st_ref[b] = v
            wt[b] = (v * w).astype(BF16)

        for k in range(SUB // SUBW):
            wgo(True, 1, sub * (SUB // SUBW) + k)
            wgo(False, 1, sub * (SUB // SUBW) + k)
    to_sibling(0)
    keep = pltpu.make_async_copy(wt, w_ref.at[mine], own_sem)
    keep.start()

    @pl.loop(0, 16)
    def _(b):
        v = st_ref[b]
        gram[...] += lax.dot_general(v, v, NT, precision=HIGH, preferred_element_type=F32)

    def side():
        for _ in gram_steps(
            at, gram, whole, half, from_sib, over_z, piece, over_xy, total, gram_sems
        ):
            yield
            yield
        yield from eliminate(terms, whole, linv_ref, work, pivots)

    aside = side()
    next(aside)
    order = (4, 5, 6, 7, 0, 1, 2, 3)
    for hop in (2, 3, 4):
        for n, sub in enumerate(order):
            wcopy(True, hop - 1, sub).wait_recv()
            if hop < 4 or sub < NW // 2:
                wgo(True, hop, sub)
            wcopy(False, hop - 1, sub).wait_recv()
            if hop < 4 or sub >= NW // 2:
                wgo(False, hop, sub)
            next(aside, None)
        to_sibling(hop - 1)
        to_sibling(NZ - (hop - 1))
    for _ in aside:
        pass
    for sub in range(NW // 2):
        wcopy(True, 4, sub).wait_recv()
        wcopy(False, 4, sub + NW // 2).wait_recv()
    to_sibling(4)
    keep.wait()
    for c in passed:
        c.wait()
    for c in sent:
        c.wait_send()


def front(lists, tile_col, tiles, omega, idf, terms):
    dma = pltpu.SemaphoreType.DMA
    v = pltpu.VMEM
    return pl.pallas_call(
        functools.partial(front_kernel, terms),
        out_shape=(
            jax.ShapeDtypeStruct((16, 16, T, T), BF16),
            jax.ShapeDtypeStruct((16, T, T), F32),
            jax.ShapeDtypeStruct((T, T), F32),
        ),
        in_specs=[SMEM, SMEM, SMEM, SMEM, VMEM, VMEM, ANY],
        out_specs=(ANY, VMEM, VMEM),
        scratch_shapes=[
            v(tiles.shape, BF16),
            v((64, T, T), BF16),
            v((2 * PER, T, T), F32),
            v((2 * (PER + 1), T, T), F32),
            *[v((8, 16, T, T), BF16)] * 3,
            *[v((4, 16, T, T), BF16)] * 4,
            v((16, T, T), BF16),
            v((T, T), F32),
            v((T, T), F32),
            v((64, T), F32),
            v((64, T), F32),
            v((8, 8, T), F32),
            v((8, T), F32),
            v((16, 8, T), F32),
            v((64, T), F32),
            v((T, 2 * T), F32),
            v((T, T), F32),
            dma,
            dma((10, 4)), dma((10, 4)),
            dma((8,)), dma((8,)),
            *[dma((4, 4))] * 4,
            dma,
            *[dma((4, NW))] * 4,
            dma((8,)), dma((8,)),
            dma, dma, dma((7,)), dma((7,)), dma((15,)), dma((15,)), dma((7,)), dma((7,)), dma, dma,
        ],
        compiler_params=params(54, 1),
        name="front",
    )(*lists, tile_col, omega, idf.reshape(16, T), tiles)


def project_kernel(col, group, slot, live, tiles_ref, w_ref, acc, raw):
    step = pl.program_id(0)

    @pl.when(step == 0)
    def _():
        @pl.loop(0, 64)
        def _(i):
            acc[i] = jnp.zeros((T, T), F32)

    for i in range(STEP):
        r = step * STEP + i
        tile_row = jnp.concatenate([tiles_ref[i, j] for j in range(5)], axis=1)
        w = w_ref[group[r] * 16 + slot[r]]
        w = jnp.where(r < live[0], w, jnp.zeros_like(w))
        raw[i] = jnp.dot(w, tile_row, preferred_element_type=F32)
    for i in range(STEP):
        r = step * STEP + i
        for j in range(5):
            c = col[j, r]
            dev, b = c // 4, c % 4
            flow = b // 2
            u, v = dev // 4, dev % 4
            t = jnp.where(flow == 0, u * 4 + v, v * 4 + u)
            acc[flow * 32 + t * 2 + b % 2] += raw[i, :, j * T : (j + 1) * T]


def project(tiles, tile_col, strip_group, strip_slot, live_count, weighted):
    strips = tiles.shape[0]
    return pl.pallas_call(
        project_kernel,
        out_shape=jax.ShapeDtypeStruct((64, T, T), F32),
        grid=(strips // STEP,),
        in_specs=[
            SMEM,
            SMEM,
            SMEM,
            SMEM,
            pl.BlockSpec((STEP, 5, T, T), lambda i: (i, 0, 0, 0)),
            pl.BlockSpec((256, T, T), lambda i: (0, 0, 0)),
        ],
        out_specs=pl.BlockSpec((64, T, T), lambda i: (0, 0, 0)),
        scratch_shapes=[pltpu.VMEM((STEP, T, 5 * T), F32)],
        compiler_params=params(48),
        name="project",
    )(tile_col, strip_group, strip_slot, live_count, tiles, weighted.reshape(256, T, T))


def ring_sum(at, axis, own, out_refs, in_refs, send, recv, size):
    here = at[axis]
    dtype = out_refs[0].dtype
    low, high = pl.ds(0, size), pl.ds(size, size)
    r0, r1, l0, l1 = range(4)
    sent = []

    def copy(k, src, dst, right):
        return pltpu.make_async_remote_copy(
            src_ref=src,
            dst_ref=dst,
            send_sem=send.at[k],
            recv_sem=recv.at[k],
            device_id=moved(at, axis, 1 if right else -1, 4),
            device_id_type=MESH,
        )

    def fill(k, offset, target, extra=None):
        out = out_refs[k]
        base = 0 if k in (r0, l0) else offset

        @pl.loop(0, size)
        def _(b):
            v = own[target, b + offset]
            if extra is not None:
                v = v + extra[b].astype(F32)
            out[base + b] = v.astype(dtype)

    far = lax.rem(here + 2, 4)
    right, left = lax.rem(here + 1, 4), lax.rem(here + 3, 4)
    c_r0 = copy(0, out_refs[r0], in_refs[r0], True)
    c_l0 = copy(1, out_refs[l0], in_refs[l0], False)
    c_r1q = copy(2, out_refs[r1].at[high], in_refs[r1].at[high], True)
    c_l1p = copy(3, out_refs[l1].at[low], in_refs[l1].at[low], False)
    c_r1p = copy(4, out_refs[r1].at[low], in_refs[r1].at[low], True)
    c_l1q = copy(5, out_refs[l1].at[high], in_refs[l1].at[high], False)
    fill(r0, 0, far)
    c_r0.start()
    fill(l0, size, far)
    c_l0.start()
    yield
    fill(r1, size, right)
    c_r1q.start()
    fill(l1, 0, left)
    c_l1p.start()
    yield
    c_r0.wait_recv()
    fill(r1, 0, right, in_refs[r0])
    c_r1p.start()
    c_l0.wait_recv()
    fill(l1, size, left, in_refs[l0])
    c_l1q.start()
    yield
    for c in (c_r1q, c_l1p, c_r1p, c_l1q):
        c.wait_recv()
    yield
    for c in (c_r0, c_l0, c_r1q, c_l1p, c_r1p, c_l1q):
        c.wait_send()
    yield


def docs_kernel(part_ref, linv_ref, st_ref, out_ref, q_ref, *scratch):
    at = place()
    bufs1 = [scratch[0:8], scratch[8:16]]
    bufs2 = [scratch[16:24], scratch[24:32]]
    sums, final, send, recv = scratch[32:]
    greet([moved(at, "x", 1, 4), moved(at, "x", -1, 4), moved(at, "y", 1, 4), moved(at, "y", -1, 4)])
    axes = ("x", "y")
    runs = [
        ring_sum(
            at, axes[f], part_ref.at[f], bufs1[f][:4], bufs1[f][4:], send.at[f], recv.at[f], 4
        )
        for f in range(2)
    ]
    for _ in range(2):
        for run in runs:
            next(run)

    def basis(first, end):
        @pl.loop(first, end)
        def _(b):
            q_ref[pl.ds(b * T, T), :] = lax.dot_general(
                st_ref[b], linv_ref[...], (((0,), (1,)), ((), ())), precision=HIGH, preferred_element_type=F32
            )

    basis(0, 6)
    for run in runs:
        next(run)
    basis(6, 12)
    for run in runs:
        next(run)
    for f in range(2):
        in_r, in_l = bufs1[f][5], bufs1[f][7]
        here = at[axes[f]]

        @pl.loop(0, 8)
        def _(b):
            v = part_ref[f, here, b] + in_r[b].astype(F32) + in_l[b].astype(F32)
            sums[f, b // 2, b % 2] = v

    later = [
        ring_sum(
            at, axes[1 - f], sums.at[f], bufs2[f][:4], bufs2[f][4:], send.at[2 + f], recv.at[2 + f], 1
        )
        for f in range(2)
    ]
    for _ in range(2):
        for run in later:
            next(run)
    basis(12, 16)
    for _ in range(2):
        for run in later:
            next(run)
    for f in range(2):
        in_r, in_l = bufs2[f][5], bufs2[f][7]
        here = at[axes[1 - f]]
        for b in range(2):
            final[2 * f + b] = sums[f, here, b] + in_r[b].astype(F32) + in_l[b].astype(F32)
    for b in range(4):
        out_ref[:, b * T : (b + 1) * T] = jnp.dot(
            linv_ref[...], final[b], precision=HIGH, preferred_element_type=F32
        ).astype(BF16)
    for run in (*runs, *later):
        next(run)


def sum_docs(parts, linv, st):
    dma = pltpu.SemaphoreType.DMA

    def bufs(size, dtype):
        return [pltpu.VMEM((n * size, T, T), dtype) for n in (1, 2, 1, 2)] * 2

    return pl.pallas_call(
        docs_kernel,
        out_shape=(
            jax.ShapeDtypeStruct((T, 4 * T), BF16),
            jax.ShapeDtypeStruct((16 * T, T), F32),
        ),
        in_specs=[VMEM, VMEM, VMEM],
        out_specs=(VMEM, VMEM),
        scratch_shapes=[
            *bufs(4, BF16),
            *bufs(4, BF16),
            *bufs(1, BF16),
            *bufs(1, BF16),
            pltpu.VMEM((2, 4, 2, T, T), F32),
            pltpu.VMEM((4, T, T), F32),
            dma((4, 6)),
            dma((4, 6)),
        ],
        compiler_params=params(24, 4),
        name="docs_sum",
    )(parts.reshape(2, 4, 8, T, T), linv, st)


def on_device(tiles, tile_col, strip_group, strip_slot, live_count, omega, idf):
    terms = idf.shape[0] * 256
    lists = strip_lists(strip_group, strip_slot, live_count)
    tile_col = tile_col.T
    weighted, st, linv = front(lists, tile_col, tiles, omega, idf, terms)
    where = (tile_col, strip_group, strip_slot, live_count)
    doc_parts = project(tiles, *where, weighted)
    doc_factor, q_basis = sum_docs(doc_parts, linv, st)
    return q_basis, doc_factor


def solution(mesh):
    torus = Mesh(mesh.devices.reshape(8, 2, 4, 4), AXES)
    in_specs = (
        P(AXES, None, None, None),
        P(AXES, None),
        P(AXES),
        P(AXES),
        P(AXES),
        P(AXES, None),
        P(AXES),
    )
    out_specs = (P(AXES, None), P(None, AXES))
    return jax.shard_map(
        on_device, mesh=torus, in_specs=in_specs, out_specs=out_specs, check_vma=False
    )
```

```python
import functools

import jax
import jax.numpy as jnp
from jax import lax
from jax.experimental import pallas as pl
from jax.experimental.pallas import tpu as pltpu
from jax.sharding import Mesh
from jax.sharding import PartitionSpec as P

AXES = ("z", "c", "x", "y")
MESH = pl.DeviceIdType.MESH
BF16 = jnp.bfloat16
F32 = jnp.float32
T = 128
NZ = 8
HIGH = lax.Precision.HIGHEST
NT = (((1,), (1,)), ((), ()))
ANY = pl.BlockSpec(memory_space=pl.ANY)
VMEM = pl.BlockSpec(memory_space=pltpu.VMEM)
SMEM = pl.BlockSpec(memory_space=pltpu.SMEM)
MIB = 1 << 20


def place():
    return {a: lax.axis_index(a) for a in AXES}


def moved(at, axis, step, size):
    there = dict(at)
    there[axis] = lax.rem(at[axis] + (step + size), size)
    return tuple(there[a] for a in AXES)


def greet(devices):
    barrier = pltpu.get_barrier_semaphore()
    for device in devices:
        pl.semaphore_signal(barrier, inc=1, device_id=device, device_id_type=MESH)
    pl.semaphore_wait(barrier, len(devices))


def params(mib, cid=None):
    if cid is None:
        return pltpu.CompilerParams(vmem_limit_bytes=mib * MIB)
    return pltpu.CompilerParams(
        vmem_limit_bytes=mib * MIB, collective_id=cid, has_side_effects=True
    )


STEP = 8
PER = 6
NONE = 6


def lists_kernel(group, slot, live, strip, before, last, count):
    @pl.loop(0, 16)
    def _(o):
        count[o] = 0

    @pl.loop(0, 256, unroll=8)
    def _(k):
        last[k] = NONE

    @pl.loop(0, 16 * PER, unroll=8)
    def _(k):
        strip[k] = 0
        before[k] = NONE

    @pl.loop(0, live[0])
    def _(r):
        o = group[r]
        n = count[o]
        at = o * 16 + slot[r]
        strip[o * PER + n] = r
        before[o * PER + n] = last[at]
        last[at] = n
        count[o] = n + 1


def strip_lists(strip_group, strip_slot, live_count):
    ints = jnp.int32
    return pl.pallas_call(
        lists_kernel,
        out_shape=(
            jax.ShapeDtypeStruct((16 * PER,), ints),
            jax.ShapeDtypeStruct((16 * PER,), ints),
            jax.ShapeDtypeStruct((256,), ints),
        ),
        in_specs=[SMEM, SMEM, SMEM],
        out_specs=(SMEM, SMEM, SMEM),
        scratch_shapes=[pltpu.SMEM((16,), ints)],
        name="strip_lists",
    )(strip_group, strip_slot, live_count)


ORDER = (4, 3, 5, 2, 6, 1, 7, 0)
SUB = 4
SUBW = 2
NW = 8


def gather_omega(at, omega_ref, om, send, recv):
    def index(axis, step):
        there = moved(at, axis, step, 4)
        return there[2] * 4 + there[3]

    def index2(first, step1, second, step2):
        there = dict(at)
        there[first] = lax.rem(at[first] + (step1 + 4), 4)
        there[second] = lax.rem(at[second] + (step2 + 4), 4)
        return there["x"] * 4 + there["y"]

    me = at["x"] * 4 + at["y"]

    def copy(i, k, axis, step, dev, lo, n):
        part = om.at[pl.ds(dev * 4 + lo, n)]
        return pltpu.make_async_remote_copy(
            src_ref=part,
            dst_ref=part,
            send_sem=send.at[i, k],
            recv_sem=recv.at[i, k],
            device_id=moved(at, axis, step, 4),
            device_id_type=MESH,
        )

    sent = []

    def go(*args):
        c = copy(*args)
        c.start()
        sent.append(c)

    def begin(i, axis, dev, h):
        go(i, 0, axis, 1, dev, 2 * h, 2)
        go(i, 1, axis, -1, dev, 2 * h, 2)

    def got(i, k, axis, dev, lo, n):
        copy(i, k, axis, 1, dev, lo, n).wait_recv()

    turns = ((0, "x", "y"), (1, "y", "x"))
    for h, a, b in turns:
        begin(5 * h, a, me, h)
    for h, a, b in turns:
        begin(5 * h + 1, b, me, h)
    for h, a, b in turns:
        i = 5 * h
        got(i, 0, a, index(a, -1), 2 * h, 2)
        go(i, 2, a, 1, index(a, -1), 2 * h, 1)
        begin(5 * h + 2, b, index(a, -1), h)
        got(i, 1, a, index(a, 1), 2 * h, 2)
        go(i, 3, a, -1, index(a, 1), 2 * h + 1, 1)
        begin(5 * h + 3, b, index(a, 1), h)
    for h, a, b in turns:
        i = 5 * h
        got(i, 2, a, index(a, 2), 2 * h, 1)
        got(i, 3, a, index(a, 2), 2 * h + 1, 1)
        begin(5 * h + 4, b, index(a, 2), h)
    steps = ((1, 0), (2, -1), (3, 1), (4, 2))
    for k, d in steps:
        for h, a, b in turns:
            i = 5 * h + k
            got(i, 0, b, index2(a, d, b, -1), 2 * h, 2)
            go(i, 2, b, 1, index2(a, d, b, -1), 2 * h, 1)
            got(i, 1, b, index2(a, d, b, 1), 2 * h, 2)
            go(i, 3, b, -1, index2(a, d, b, 1), 2 * h + 1, 1)
    for k, d in steps:
        for h, a, b in turns:
            i = 5 * h + k
            got(i, 2, b, index2(a, d, b, 2), 2 * h, 1)
            got(i, 3, b, index2(a, d, b, 2), 2 * h + 1, 1)
    return sent


def gram_steps(at, g_ref, whole, half, from_sib, over_z, piece, over_xy, total, sems):
    z, c, x, y = (at[a] for a in AXES)
    sibling = (z, 1 - c, x, y)
    a_send, a_recv, z_send, z_recv, p_send, p_recv, b_send, b_recv, s_send, s_recv = sems

    def put(src, dst, ss, rs, device):
        cp = pltpu.make_async_remote_copy(
            src_ref=src, dst_ref=dst, send_sem=ss, recv_sem=rs, device_id=device, device_id_type=MESH
        )
        cp.start()
        return cp

    def rows(i, n):
        return pl.ds(pl.multiple_of(i * n, n), n)

    one = put(g_ref.at[rows(1 - c, 64)], from_sib, a_send, a_recv, sibling)
    yield
    one.wait()
    half[...] = g_ref[rows(c, 64), :] + from_sib[...]
    z_peers = [moved(at, "z", d, NZ) for d in range(1, NZ)]
    copies = [
        put(half.at[rows(p[0], 8)], over_z.at[z], z_send.at[d], z_recv.at[d], p)
        for d, p in enumerate(z_peers)
    ]
    over_z[z] = half[rows(z, 8), :]
    yield
    for cp in copies:
        cp.wait()
    piece[...] = functools.reduce(lambda u, v: u + v, [over_z[i] for i in range(NZ)])
    me = x * 4 + y
    copies = [
        put(piece, over_xy.at[me], p_send.at[d], p_recv.at[d], p) for d, p in enumerate(xy_others(at))
    ]
    over_xy[me] = piece[...]
    yield
    for cp in copies:
        cp.wait()
    total[rows(z, 8), :] = functools.reduce(lambda u, v: u + v, [over_xy[i] for i in range(16)])
    copies = [
        put(total.at[rows(z, 8)], total.at[rows(z, 8)], b_send.at[d], b_recv.at[d], p)
        for d, p in enumerate(z_peers)
    ]
    yield
    for cp in copies:
        cp.wait()
    one = put(total, whole.at[rows(c, 64)], s_send, s_recv, sibling)
    whole[rows(c, 64), :] = total[...]
    yield
    one.wait()
    yield


def xy_others(at):
    z, c, x, y = (at[a] for a in AXES)
    return [(z, c, lax.rem(x + i, 4), lax.rem(y + j, 4)) for i in range(4) for j in range(4) if i or j]


def eliminate(terms, gram, linv_ref, work):
    work[...] = gram[...] * (1.0 / terms)
    row = lax.broadcasted_iota(jnp.int32, (T, T), 0)
    lane = lax.broadcasted_iota(jnp.int32, (T, T), 1)
    for first in range(0, T, 8):

        @pl.loop(first, first + 8)
        def _(j):
            here = lane == j
            line = work[pl.ds(j, 1), :]
            pivot = jnp.sum(jnp.where(here[:1], line, 0.0), axis=1, keepdims=True)
            scaled = jnp.where(here[:1], 1.0, line) / pivot
            block = work[...]
            column = jnp.sum(jnp.where(here, block, 0.0), axis=1, keepdims=True)
            below = row > j
            work[...] = jnp.where(here & below, 0.0, block) - jnp.where(below, column, 0.0) * scaled

        yield
    block = work[...]
    pivots = jnp.sum(jnp.where(lane == row, block, 0.0), axis=1, keepdims=True)
    linv_ref[...] = jnp.where(lane < row, block, (lane == row).astype(F32)) * lax.rsqrt(pivots)
    yield


def front_kernel(
    terms, strip, before, last, col, omega_ref, idf_ref, tiles_ref, w_ref, st_ref, linv_ref,
    tiles, om, raw, chain, own, out_sib, sib, out_r, out_l, in_r, in_l, wt, gram,
    whole, half, from_sib, over_z, piece, over_xy, total, work,
    load_sem, om_send, om_recv, sib_send, sib_recv, r_send, r_recv, l_send, l_recv,
    own_sem, wr_send, wr_recv, wl_send, wl_recv, ws_send, ws_recv, *gram_sems,
):
    at = place()
    load = pltpu.make_async_copy(tiles_ref, tiles, load_sem)
    load.start()
    sibling = (at["z"], 1 - at["c"], at["x"], at["y"])
    me = at["x"] * 4 + at["y"]
    for b in range(4):
        om[me * 4 + b] = omega_ref[b * T : (b + 1) * T, :].T
    near = [moved(at, a, d, 4) for a in ("x", "y") for d in (1, -1)]
    greet([sibling, *near, moved(at, "z", 1, NZ), moved(at, "z", -1, NZ)])
    sent = gather_omega(at, omega_ref, om, om_send, om_recv)

    @pl.loop(0, 2 * (PER + 1))
    def _(k):
        chain[k] = jnp.zeros((T, T), F32)

    load.wait()
    slot_of = {d: q for q, d in enumerate(ORDER)}

    def sketch(d):
        q = slot_of[d]
        z = lax.rem(at["z"] + d, NZ)
        for k, target in ((0, out_sib), (1, own)):
            o = 2 * z + (1 - at["c"] if k == 0 else at["c"])
            base = k * (PER + 1)

            @pl.loop(0, PER, unroll=3)
            def _(n):
                i = strip[o * PER + n]
                tile_row = jnp.concatenate([tiles[i, j] for j in range(5)], axis=1)
                m = jnp.concatenate([om[col[j, i]] for j in range(5)], axis=1)
                raw[k * PER + n] = lax.dot_general(m, tile_row, NT, preferred_element_type=F32)

            @pl.loop(0, PER)
            def _(n):
                chain[base + n] = raw[k * PER + n] + chain[base + before[o * PER + n]]

            @pl.loop(0, 16, unroll=2)
            def _(b):
                target[q, b] = chain[base + last[o * 16 + b]].astype(BF16)

            if k == 0:
                c = pltpu.make_async_remote_copy(
                    src_ref=out_sib.at[q],
                    dst_ref=sib.at[q],
                    send_sem=sib_send.at[q],
                    recv_sem=sib_recv.at[q],
                    device_id=sibling,
                    device_id_type=MESH,
                )
                c.start()
        sent.append(c)
        theirs[q] = c

    theirs = {}
    ready = set()

    def need(q):
        if q not in ready:
            ready.add(q)
            theirs[q].wait_recv()

    def copy(right, s, sub):
        rows = pl.ds(sub * SUB, SUB)
        return pltpu.make_async_remote_copy(
            src_ref=(out_r if right else out_l).at[s, rows],
            dst_ref=(in_r if right else in_l).at[s, rows],
            send_sem=(r_send if right else l_send).at[s, sub],
            recv_sem=(r_recv if right else l_recv).at[s, sub],
            device_id=moved(at, "z", 1 if right else -1, NZ),
            device_id_type=MESH,
        )

    def send(right, s, sub, add):
        d = (4 - s) if right else (4 + s)
        q = slot_of[d]
        need(q)
        if add:
            copy(right, s - 1, sub).wait_recv()

        @pl.loop(sub * SUB, (sub + 1) * SUB)
        def _(b):
            v = own[q, b].astype(F32) + sib[q, b].astype(F32)
            if add:
                v = v + (in_r if right else in_l)[s - 1, b].astype(F32)
            (out_r if right else out_l)[s, b] = v.astype(BF16)

        c = copy(right, s, sub)
        c.start()
        sent.append(c)

    sketch(4)
    for sub in (0, 1):
        send(True, 0, sub, False)
        send(False, 0, sub + 2, False)
    sketch(3)
    sketch(5)
    for sub in (0, 1):
        send(True, 1, sub + 2, False)
        send(False, 1, sub, False)
    for sub in (0, 1):
        send(True, 1, sub, True)
        send(False, 1, sub + 2, True)
    sketch(2)
    sketch(6)
    for s in (2, 3):
        for sub in (2, 3, 0, 1):
            send(True, s, sub, True)
            send(False, s, (sub + 2) % 4, True)
        if s == 2:
            sketch(1)
            sketch(7)
    sketch(0)

    mine = 2 * at["z"] + at["c"]

    def wcopy(right, hop, sub):
        owner = 2 * lax.rem(at["z"] + ((1 - hop) if right else (hop - 1)) + NZ, NZ) + at["c"]
        rows = pl.ds(sub * SUBW, SUBW)
        return pltpu.make_async_remote_copy(
            src_ref=wt.at[rows] if hop == 1 else w_ref.at[owner, rows],
            dst_ref=w_ref.at[owner, rows],
            send_sem=(wr_send if right else wl_send).at[hop - 1, sub],
            recv_sem=(wr_recv if right else wl_recv).at[hop - 1, sub],
            device_id=moved(at, "z", 1 if right else -1, NZ),
            device_id_type=MESH,
        )

    def wgo(right, hop, sub):
        c = wcopy(right, hop, sub)
        c.start()
        sent.append(c)

    def to_sibling(d):
        owner = 2 * lax.rem(at["z"] + d, NZ) + at["c"]
        c = pltpu.make_async_remote_copy(
            src_ref=wt if d == 0 else w_ref.at[owner],
            dst_ref=w_ref.at[owner],
            send_sem=ws_send.at[d],
            recv_sem=ws_recv.at[d],
            device_id=sibling,
            device_id_type=MESH,
        )
        c.start()
        passed.append(c)

    passed = []
    q = slot_of[0]
    need(q)
    gram[...] = jnp.zeros((T, T), F32)
    for sub in (2, 3, 0, 1):
        copy(True, 3, sub).wait_recv()
        copy(False, 3, sub).wait_recv()

        @pl.loop(sub * SUB, (sub + 1) * SUB)
        def _(b):
            v = own[q, b].astype(F32) + sib[q, b].astype(F32)
            v = v + in_r[3, b].astype(F32) + in_l[3, b].astype(F32)
            w = idf_ref[pl.ds(b, 1), :]
            v = v * w
            st_ref[b] = v
            wt[b] = (v * w).astype(BF16)

        for k in range(SUB // SUBW):
            wgo(True, 1, sub * (SUB // SUBW) + k)
            wgo(False, 1, sub * (SUB // SUBW) + k)
    to_sibling(0)
    keep = pltpu.make_async_copy(wt, w_ref.at[mine], own_sem)
    keep.start()

    @pl.loop(0, 16)
    def _(b):
        v = st_ref[b]
        gram[...] += lax.dot_general(v, v, NT, precision=HIGH, preferred_element_type=F32)

    def side():
        for _ in gram_steps(
            at, gram, whole, half, from_sib, over_z, piece, over_xy, total, gram_sems
        ):
            yield
            yield
        yield from eliminate(terms, whole, linv_ref, work)

    aside = side()
    next(aside)
    order = (4, 5, 6, 7, 0, 1, 2, 3)
    for hop in (2, 3, 4):
        for n, sub in enumerate(order):
            wcopy(True, hop - 1, sub).wait_recv()
            if hop < 4 or sub < NW // 2:
                wgo(True, hop, sub)
            wcopy(False, hop - 1, sub).wait_recv()
            if hop < 4 or sub >= NW // 2:
                wgo(False, hop, sub)
            next(aside, None)
        to_sibling(hop - 1)
        to_sibling(NZ - (hop - 1))
    for _ in aside:
        pass
    for sub in range(NW // 2):
        wcopy(True, 4, sub).wait_recv()
        wcopy(False, 4, sub + NW // 2).wait_recv()
    to_sibling(4)
    keep.wait()
    for c in passed:
        c.wait()
    for c in sent:
        c.wait_send()


def front(lists, tile_col, tiles, omega, idf, terms):
    dma = pltpu.SemaphoreType.DMA
    v = pltpu.VMEM
    return pl.pallas_call(
        functools.partial(front_kernel, terms),
        out_shape=(
            jax.ShapeDtypeStruct((16, 16, T, T), BF16),
            jax.ShapeDtypeStruct((16, T, T), F32),
            jax.ShapeDtypeStruct((T, T), F32),
        ),
        in_specs=[SMEM, SMEM, SMEM, SMEM, VMEM, VMEM, ANY],
        out_specs=(ANY, VMEM, VMEM),
        scratch_shapes=[
            v(tiles.shape, BF16),
            v((64, T, T), BF16),
            v((2 * PER, T, T), F32),
            v((2 * (PER + 1), T, T), F32),
            *[v((8, 16, T, T), BF16)] * 3,
            *[v((4, 16, T, T), BF16)] * 4,
            v((16, T, T), BF16),
            v((T, T), F32),
            v((T, T), F32),
            v((64, T), F32),
            v((64, T), F32),
            v((8, 8, T), F32),
            v((8, T), F32),
            v((16, 8, T), F32),
            v((64, T), F32),
            v((T, T), F32),
            dma,
            dma((10, 4)), dma((10, 4)),
            dma((8,)), dma((8,)),
            *[dma((4, 4))] * 4,
            dma,
            *[dma((4, NW))] * 4,
            dma((8,)), dma((8,)),
            dma, dma, dma((7,)), dma((7,)), dma((15,)), dma((15,)), dma((7,)), dma((7,)), dma, dma,
        ],
        compiler_params=params(54, 1),
        name="front",
    )(*lists, tile_col, omega, idf.reshape(16, T), tiles)


def project_kernel(col, group, slot, live, tiles_ref, w_ref, acc, raw, blocks, sem):
    step = pl.program_id(0)

    def fetch(step):
        at = step % 2
        copies = []
        for i in range(STEP):
            r = step * STEP + i
            copies.append(
                pltpu.make_async_copy(
                    w_ref.at[group[r] * 16 + slot[r]], blocks.at[at, i], sem.at[at, i]
                )
            )
        return copies

    @pl.when(step == 0)
    def _():
        for c in fetch(step):
            c.start()

    @pl.when(step + 1 < pl.num_programs(0))
    def _():
        for c in fetch(step + 1):
            c.start()

    @pl.when(step == 0)
    def _():
        @pl.loop(0, 64)
        def _(i):
            acc[i] = jnp.zeros((T, T), F32)

    for c in fetch(step):
        c.wait()
    for i in range(STEP):
        r = step * STEP + i
        tile_row = jnp.concatenate([tiles_ref[i, j] for j in range(5)], axis=1)
        w = blocks[step % 2, i]
        w = jnp.where(r < live[0], w, jnp.zeros_like(w))
        raw[i] = jnp.dot(w, tile_row, preferred_element_type=F32)
    for i in range(STEP):
        r = step * STEP + i
        for j in range(5):
            c = col[j, r]
            dev, b = c // 4, c % 4
            flow = b // 2
            u, v = dev // 4, dev % 4
            t = jnp.where(flow == 0, u * 4 + v, v * 4 + u)
            acc[flow * 32 + t * 2 + b % 2] += raw[i, :, j * T : (j + 1) * T]


def project(tiles, tile_col, strip_group, strip_slot, live_count, weighted):
    strips = tiles.shape[0]
    return pl.pallas_call(
        project_kernel,
        out_shape=jax.ShapeDtypeStruct((64, T, T), F32),
        grid=(strips // STEP,),
        in_specs=[
            SMEM,
            SMEM,
            SMEM,
            SMEM,
            pl.BlockSpec((STEP, 5, T, T), lambda i: (i, 0, 0, 0)),
            ANY,
        ],
        out_specs=pl.BlockSpec((64, T, T), lambda i: (0, 0, 0)),
        scratch_shapes=[
            pltpu.VMEM((STEP, T, 5 * T), F32),
            pltpu.VMEM((2, STEP, T, T), BF16),
            pltpu.SemaphoreType.DMA((2, STEP)),
        ],
        compiler_params=params(48),
        name="project",
    )(tile_col, strip_group, strip_slot, live_count, tiles, weighted.reshape(256, T, T))


def ring_sum(at, axis, own, out_refs, in_refs, send, recv, size):
    here = at[axis]
    dtype = out_refs[0].dtype
    low, high = pl.ds(0, size), pl.ds(size, size)
    r0, r1, l0, l1 = range(4)
    sent = []

    def copy(k, src, dst, right):
        return pltpu.make_async_remote_copy(
            src_ref=src,
            dst_ref=dst,
            send_sem=send.at[k],
            recv_sem=recv.at[k],
            device_id=moved(at, axis, 1 if right else -1, 4),
            device_id_type=MESH,
        )

    def fill(k, offset, target, extra=None):
        out = out_refs[k]
        base = 0 if k in (r0, l0) else offset

        @pl.loop(0, size)
        def _(b):
            v = own[target, b + offset]
            if extra is not None:
                v = v + extra[b].astype(F32)
            out[base + b] = v.astype(dtype)

    far = lax.rem(here + 2, 4)
    right, left = lax.rem(here + 1, 4), lax.rem(here + 3, 4)
    c_r0 = copy(0, out_refs[r0], in_refs[r0], True)
    c_l0 = copy(1, out_refs[l0], in_refs[l0], False)
    c_r1q = copy(2, out_refs[r1].at[high], in_refs[r1].at[high], True)
    c_l1p = copy(3, out_refs[l1].at[low], in_refs[l1].at[low], False)
    c_r1p = copy(4, out_refs[r1].at[low], in_refs[r1].at[low], True)
    c_l1q = copy(5, out_refs[l1].at[high], in_refs[l1].at[high], False)
    fill(r0, 0, far)
    c_r0.start()
    fill(l0, size, far)
    c_l0.start()
    yield
    fill(r1, size, right)
    c_r1q.start()
    fill(l1, 0, left)
    c_l1p.start()
    yield
    c_r0.wait_recv()
    fill(r1, 0, right, in_refs[r0])
    c_r1p.start()
    c_l0.wait_recv()
    fill(l1, size, left, in_refs[l0])
    c_l1q.start()
    yield
    for c in (c_r1q, c_l1p, c_r1p, c_l1q):
        c.wait_recv()
    yield
    for c in (c_r0, c_l0, c_r1q, c_l1p, c_r1p, c_l1q):
        c.wait_send()
    yield


def docs_kernel(part_ref, linv_ref, st_ref, out_ref, q_ref, *scratch):
    at = place()
    bufs1 = [scratch[0:8], scratch[8:16]]
    bufs2 = [scratch[16:24], scratch[24:32]]
    sums, final, send, recv = scratch[32:]
    greet([moved(at, "x", 1, 4), moved(at, "x", -1, 4), moved(at, "y", 1, 4), moved(at, "y", -1, 4)])
    axes = ("x", "y")
    runs = [
        ring_sum(
            at, axes[f], part_ref.at[f], bufs1[f][:4], bufs1[f][4:], send.at[f], recv.at[f], 4
        )
        for f in range(2)
    ]
    for _ in range(2):
        for run in runs:
            next(run)

    def basis(first, end):
        @pl.loop(first, end)
        def _(b):
            q_ref[pl.ds(b * T, T), :] = lax.dot_general(
                st_ref[b], linv_ref[...], (((0,), (1,)), ((), ())), precision=HIGH, preferred_element_type=F32
            )

    basis(0, 6)
    for run in runs:
        next(run)
    basis(6, 12)
    for run in runs:
        next(run)
    for f in range(2):
        in_r, in_l = bufs1[f][5], bufs1[f][7]
        here = at[axes[f]]

        @pl.loop(0, 8)
        def _(b):
            v = part_ref[f, here, b] + in_r[b].astype(F32) + in_l[b].astype(F32)
            sums[f, b // 2, b % 2] = v

    later = [
        ring_sum(
            at, axes[1 - f], sums.at[f], bufs2[f][:4], bufs2[f][4:], send.at[2 + f], recv.at[2 + f], 1
        )
        for f in range(2)
    ]
    for _ in range(2):
        for run in later:
            next(run)
    basis(12, 16)
    for _ in range(2):
        for run in later:
            next(run)
    for f in range(2):
        in_r, in_l = bufs2[f][5], bufs2[f][7]
        here = at[axes[1 - f]]
        for b in range(2):
            final[2 * f + b] = sums[f, here, b] + in_r[b].astype(F32) + in_l[b].astype(F32)
    for b in range(4):
        out_ref[:, b * T : (b + 1) * T] = jnp.dot(
            linv_ref[...], final[b], precision=HIGH, preferred_element_type=F32
        ).astype(BF16)
    for run in (*runs, *later):
        next(run)


def sum_docs(parts, linv, st):
    dma = pltpu.SemaphoreType.DMA

    def bufs(size, dtype):
        return [pltpu.VMEM((n * size, T, T), dtype) for n in (1, 2, 1, 2)] * 2

    return pl.pallas_call(
        docs_kernel,
        out_shape=(
            jax.ShapeDtypeStruct((T, 4 * T), BF16),
            jax.ShapeDtypeStruct((16 * T, T), F32),
        ),
        in_specs=[VMEM, VMEM, VMEM],
        out_specs=(VMEM, VMEM),
        scratch_shapes=[
            *bufs(4, BF16),
            *bufs(4, BF16),
            *bufs(1, BF16),
            *bufs(1, BF16),
            pltpu.VMEM((2, 4, 2, T, T), F32),
            pltpu.VMEM((4, T, T), F32),
            dma((4, 6)),
            dma((4, 6)),
        ],
        compiler_params=params(24, 4),
        name="docs_sum",
    )(parts.reshape(2, 4, 8, T, T), linv, st)


def on_device(tiles, tile_col, strip_group, strip_slot, live_count, omega, idf):
    terms = idf.shape[0] * 256
    lists = strip_lists(strip_group, strip_slot, live_count)
    tile_col = tile_col.T
    weighted, st, linv = front(lists, tile_col, tiles, omega, idf, terms)
    where = (tile_col, strip_group, strip_slot, live_count)
    doc_parts = project(tiles, *where, weighted)
    doc_factor, q_basis = sum_docs(doc_parts, linv, st)
    return q_basis, doc_factor


def solution(mesh):
    torus = Mesh(mesh.devices.reshape(8, 2, 4, 4), AXES)
    in_specs = (
        P(AXES, None, None, None),
        P(AXES, None),
        P(AXES),
        P(AXES),
        P(AXES),
        P(AXES, None),
        P(AXES),
    )
    out_specs = (P(AXES, None), P(None, AXES))
    return jax.shard_map(
        on_device, mesh=torus, in_specs=in_specs, out_specs=out_specs, check_vma=False
    )
```

```python
import functools

import jax
import jax.numpy as jnp
from jax import lax
from jax.experimental import pallas as pl
from jax.experimental.pallas import tpu as pltpu
from jax.sharding import Mesh
from jax.sharding import PartitionSpec as P

AXES = ("z", "c", "x", "y")
MESH = pl.DeviceIdType.MESH
BF16 = jnp.bfloat16
F32 = jnp.float32
T = 128
NZ = 8
HIGH = lax.Precision.HIGHEST
NT = (((1,), (1,)), ((), ()))
ANY = pl.BlockSpec(memory_space=pl.ANY)
VMEM = pl.BlockSpec(memory_space=pltpu.VMEM)
SMEM = pl.BlockSpec(memory_space=pltpu.SMEM)
MIB = 1 << 20


def place():
    return {a: lax.axis_index(a) for a in AXES}


def moved(at, axis, step, size):
    there = dict(at)
    there[axis] = lax.rem(at[axis] + (step + size), size)
    return tuple(there[a] for a in AXES)


def greet(devices):
    barrier = pltpu.get_barrier_semaphore()
    for device in devices:
        pl.semaphore_signal(barrier, inc=1, device_id=device, device_id_type=MESH)
    pl.semaphore_wait(barrier, len(devices))


def params(mib, cid=None):
    if cid is None:
        return pltpu.CompilerParams(vmem_limit_bytes=mib * MIB)
    return pltpu.CompilerParams(
        vmem_limit_bytes=mib * MIB, collective_id=cid, has_side_effects=True
    )


STEP = 12
PER = 6
NONE = 6


def lists_kernel(group, slot, live, strip, before, last, count):
    @pl.loop(0, 16)
    def _(o):
        count[o] = 0

    @pl.loop(0, 256, unroll=8)
    def _(k):
        last[k] = NONE

    @pl.loop(0, 16 * PER, unroll=8)
    def _(k):
        strip[k] = 0
        before[k] = NONE

    @pl.loop(0, live[0])
    def _(r):
        o = group[r]
        n = count[o]
        at = o * 16 + slot[r]
        strip[o * PER + n] = r
        before[o * PER + n] = last[at]
        last[at] = n
        count[o] = n + 1


def strip_lists(strip_group, strip_slot, live_count):
    ints = jnp.int32
    return pl.pallas_call(
        lists_kernel,
        out_shape=(
            jax.ShapeDtypeStruct((16 * PER,), ints),
            jax.ShapeDtypeStruct((16 * PER,), ints),
            jax.ShapeDtypeStruct((256,), ints),
        ),
        in_specs=[SMEM, SMEM, SMEM],
        out_specs=(SMEM, SMEM, SMEM),
        scratch_shapes=[pltpu.SMEM((16,), ints)],
        name="strip_lists",
    )(strip_group, strip_slot, live_count)


ORDER = (4, 3, 5, 2, 6, 1, 7, 0)
SUB = 4
SUBW = 4
NW = 4


def gather_omega(at, omega_ref, om, send, recv):
    def index(axis, step):
        there = moved(at, axis, step, 4)
        return there[2] * 4 + there[3]

    def index2(first, step1, second, step2):
        there = dict(at)
        there[first] = lax.rem(at[first] + (step1 + 4), 4)
        there[second] = lax.rem(at[second] + (step2 + 4), 4)
        return there["x"] * 4 + there["y"]

    me = at["x"] * 4 + at["y"]

    def copy(i, k, axis, step, dev, lo, n):
        part = om.at[pl.ds(dev * 4 + lo, n)]
        return pltpu.make_async_remote_copy(
            src_ref=part,
            dst_ref=part,
            send_sem=send.at[i, k],
            recv_sem=recv.at[i, k],
            device_id=moved(at, axis, step, 4),
            device_id_type=MESH,
        )

    sent = []

    def go(*args):
        c = copy(*args)
        c.start()
        sent.append(c)

    def begin(i, axis, dev, h):
        go(i, 0, axis, 1, dev, 2 * h, 2)
        go(i, 1, axis, -1, dev, 2 * h, 2)

    def got(i, k, axis, dev, lo, n):
        copy(i, k, axis, 1, dev, lo, n).wait_recv()

    turns = ((0, "x", "y"), (1, "y", "x"))
    for h, a, b in turns:
        begin(5 * h, a, me, h)
    for h, a, b in turns:
        begin(5 * h + 1, b, me, h)
    for h, a, b in turns:
        i = 5 * h
        got(i, 0, a, index(a, -1), 2 * h, 2)
        go(i, 2, a, 1, index(a, -1), 2 * h, 1)
        begin(5 * h + 2, b, index(a, -1), h)
        got(i, 1, a, index(a, 1), 2 * h, 2)
        go(i, 3, a, -1, index(a, 1), 2 * h + 1, 1)
        begin(5 * h + 3, b, index(a, 1), h)
    for h, a, b in turns:
        i = 5 * h
        got(i, 2, a, index(a, 2), 2 * h, 1)
        got(i, 3, a, index(a, 2), 2 * h + 1, 1)
        begin(5 * h + 4, b, index(a, 2), h)
    steps = ((1, 0), (2, -1), (3, 1), (4, 2))
    for k, d in steps:
        for h, a, b in turns:
            i = 5 * h + k
            got(i, 0, b, index2(a, d, b, -1), 2 * h, 2)
            go(i, 2, b, 1, index2(a, d, b, -1), 2 * h, 1)
            got(i, 1, b, index2(a, d, b, 1), 2 * h, 2)
            go(i, 3, b, -1, index2(a, d, b, 1), 2 * h + 1, 1)
    for k, d in steps:
        for h, a, b in turns:
            i = 5 * h + k
            got(i, 2, b, index2(a, d, b, 2), 2 * h, 1)
            got(i, 3, b, index2(a, d, b, 2), 2 * h + 1, 1)
    return sent


def gram_steps(at, g_ref, whole, half, from_sib, over_z, piece, over_xy, total, sems):
    z, c, x, y = (at[a] for a in AXES)
    sibling = (z, 1 - c, x, y)
    a_send, a_recv, z_send, z_recv, p_send, p_recv, b_send, b_recv, s_send, s_recv = sems

    def put(src, dst, ss, rs, device):
        cp = pltpu.make_async_remote_copy(
            src_ref=src, dst_ref=dst, send_sem=ss, recv_sem=rs, device_id=device, device_id_type=MESH
        )
        cp.start()
        return cp

    def rows(i, n):
        return pl.ds(pl.multiple_of(i * n, n), n)

    one = put(g_ref.at[rows(1 - c, 64)], from_sib, a_send, a_recv, sibling)
    yield
    one.wait()
    half[...] = g_ref[rows(c, 64), :] + from_sib[...]
    z_peers = [moved(at, "z", d, NZ) for d in range(1, NZ)]
    copies = [
        put(half.at[rows(p[0], 8)], over_z.at[z], z_send.at[d], z_recv.at[d], p)
        for d, p in enumerate(z_peers)
    ]
    over_z[z] = half[rows(z, 8), :]
    yield
    for cp in copies:
        cp.wait()
    piece[...] = functools.reduce(lambda u, v: u + v, [over_z[i] for i in range(NZ)])
    me = x * 4 + y
    copies = [
        put(piece, over_xy.at[me], p_send.at[d], p_recv.at[d], p) for d, p in enumerate(xy_others(at))
    ]
    over_xy[me] = piece[...]
    yield
    for cp in copies:
        cp.wait()
    total[rows(z, 8), :] = functools.reduce(lambda u, v: u + v, [over_xy[i] for i in range(16)])
    copies = [
        put(total.at[rows(z, 8)], total.at[rows(z, 8)], b_send.at[d], b_recv.at[d], p)
        for d, p in enumerate(z_peers)
    ]
    yield
    for cp in copies:
        cp.wait()
    one = put(total, whole.at[rows(c, 64)], s_send, s_recv, sibling)
    whole[rows(c, 64), :] = total[...]
    yield
    one.wait()
    yield


def xy_others(at):
    z, c, x, y = (at[a] for a in AXES)
    return [(z, c, lax.rem(x + i, 4), lax.rem(y + j, 4)) for i in range(4) for j in range(4) if i or j]


def eliminate(terms, gram, linv_ref, work):
    work[...] = gram[...] * (1.0 / terms)
    row = lax.broadcasted_iota(jnp.int32, (T, T), 0)
    lane = lax.broadcasted_iota(jnp.int32, (T, T), 1)
    for first in range(0, T, 8):

        @pl.loop(first, first + 8)
        def _(j):
            here = lane == j
            line = work[pl.ds(j, 1), :]
            pivot = jnp.sum(jnp.where(here[:1], line, 0.0), axis=1, keepdims=True)
            scaled = jnp.where(here[:1], 1.0, line) / pivot
            block = work[...]
            column = jnp.sum(jnp.where(here, block, 0.0), axis=1, keepdims=True)
            below = row > j
            work[...] = jnp.where(here & below, 0.0, block) - jnp.where(below, column, 0.0) * scaled

        yield
    block = work[...]
    pivots = jnp.sum(jnp.where(lane == row, block, 0.0), axis=1, keepdims=True)
    linv_ref[...] = jnp.where(lane < row, block, (lane == row).astype(F32)) * lax.rsqrt(pivots)
    yield


def front_kernel(
    terms, strip, before, last, col, omega_ref, idf_ref, tiles_ref, w_ref, st_ref, linv_ref,
    tiles, om, raw, chain, own, out_sib, sib, out_r, out_l, in_r, in_l, wt, gram,
    whole, half, from_sib, over_z, piece, over_xy, total, work,
    load_sem, om_send, om_recv, sib_send, sib_recv, r_send, r_recv, l_send, l_recv,
    own_sem, wr_send, wr_recv, wl_send, wl_recv, ws_send, ws_recv, *gram_sems,
):
    at = place()
    load = pltpu.make_async_copy(tiles_ref, tiles, load_sem)
    load.start()
    sibling = (at["z"], 1 - at["c"], at["x"], at["y"])
    me = at["x"] * 4 + at["y"]
    for b in range(4):
        om[me * 4 + b] = omega_ref[b * T : (b + 1) * T, :].T
    near = [moved(at, a, d, 4) for a in ("x", "y") for d in (1, -1)]
    greet([sibling, *near, moved(at, "z", 1, NZ), moved(at, "z", -1, NZ)])
    sent = gather_omega(at, omega_ref, om, om_send, om_recv)

    @pl.loop(0, 2 * (PER + 1))
    def _(k):
        chain[k] = jnp.zeros((T, T), F32)

    load.wait()
    slot_of = {d: q for q, d in enumerate(ORDER)}

    def sketch(d):
        q = slot_of[d]
        z = lax.rem(at["z"] + d, NZ)
        for k, target in ((0, out_sib), (1, own)):
            o = 2 * z + (1 - at["c"] if k == 0 else at["c"])
            base = k * (PER + 1)

            @pl.loop(0, PER, unroll=6)
            def _(n):
                i = strip[o * PER + n]
                tile_row = jnp.concatenate([tiles[i, j] for j in range(5)], axis=1)
                m = jnp.concatenate([om[col[j, i]] for j in range(5)], axis=1)
                raw[k * PER + n] = lax.dot_general(m, tile_row, NT, preferred_element_type=F32)

            @pl.loop(0, PER, unroll=2)
            def _(n):
                chain[base + n] = raw[k * PER + n] + chain[base + before[o * PER + n]]

            @pl.loop(0, 16, unroll=4)
            def _(b):
                target[q, b] = chain[base + last[o * 16 + b]].astype(BF16)

            if k == 0:
                c = pltpu.make_async_remote_copy(
                    src_ref=out_sib.at[q],
                    dst_ref=sib.at[q],
                    send_sem=sib_send.at[q],
                    recv_sem=sib_recv.at[q],
                    device_id=sibling,
                    device_id_type=MESH,
                )
                c.start()
        sent.append(c)
        theirs[q] = c

    theirs = {}
    ready = set()

    def need(q):
        if q not in ready:
            ready.add(q)
            theirs[q].wait_recv()

    def copy(right, s, sub):
        rows = pl.ds(sub * SUB, SUB)
        return pltpu.make_async_remote_copy(
            src_ref=(out_r if right else out_l).at[s, rows],
            dst_ref=(in_r if right else in_l).at[s, rows],
            send_sem=(r_send if right else l_send).at[s, sub],
            recv_sem=(r_recv if right else l_recv).at[s, sub],
            device_id=moved(at, "z", 1 if right else -1, NZ),
            device_id_type=MESH,
        )

    def send(right, s, sub, add):
        d = (4 - s) if right else (4 + s)
        q = slot_of[d]
        need(q)
        if add:
            copy(right, s - 1, sub).wait_recv()

        @pl.loop(sub * SUB, (sub + 1) * SUB)
        def _(b):
            v = own[q, b].astype(F32) + sib[q, b].astype(F32)
            if add:
                v = v + (in_r if right else in_l)[s - 1, b].astype(F32)
            (out_r if right else out_l)[s, b] = v.astype(BF16)

        c = copy(right, s, sub)
        c.start()
        sent.append(c)

    sketch(4)
    for sub in (0, 1):
        send(True, 0, sub, False)
        send(False, 0, sub + 2, False)
    sketch(3)
    sketch(5)
    for sub in (0, 1):
        send(True, 1, sub + 2, False)
        send(False, 1, sub, False)
    for sub in (0, 1):
        send(True, 1, sub, True)
        send(False, 1, sub + 2, True)
    sketch(2)
    sketch(6)
    for s in (2, 3):
        for sub in (2, 3, 0, 1):
            send(True, s, sub, True)
            send(False, s, (sub + 2) % 4, True)
        if s == 2:
            sketch(1)
            sketch(7)
    sketch(0)

    mine = 2 * at["z"] + at["c"]

    def wcopy(right, hop, sub):
        owner = 2 * lax.rem(at["z"] + ((1 - hop) if right else (hop - 1)) + NZ, NZ) + at["c"]
        rows = pl.ds(sub * SUBW, SUBW)
        return pltpu.make_async_remote_copy(
            src_ref=wt.at[rows] if hop == 1 else w_ref.at[owner, rows],
            dst_ref=w_ref.at[owner, rows],
            send_sem=(wr_send if right else wl_send).at[hop - 1, sub],
            recv_sem=(wr_recv if right else wl_recv).at[hop - 1, sub],
            device_id=moved(at, "z", 1 if right else -1, NZ),
            device_id_type=MESH,
        )

    def wgo(right, hop, sub):
        c = wcopy(right, hop, sub)
        c.start()
        sent.append(c)

    def to_sibling(d):
        owner = 2 * lax.rem(at["z"] + d, NZ) + at["c"]
        c = pltpu.make_async_remote_copy(
            src_ref=wt if d == 0 else w_ref.at[owner],
            dst_ref=w_ref.at[owner],
            send_sem=ws_send.at[d],
            recv_sem=ws_recv.at[d],
            device_id=sibling,
            device_id_type=MESH,
        )
        c.start()
        passed.append(c)

    passed = []
    q = slot_of[0]
    need(q)
    gram[...] = jnp.zeros((T, T), F32)
    for sub in (2, 3, 0, 1):
        copy(True, 3, sub).wait_recv()
        copy(False, 3, sub).wait_recv()

        @pl.loop(sub * SUB, (sub + 1) * SUB)
        def _(b):
            v = own[q, b].astype(F32) + sib[q, b].astype(F32)
            v = v + in_r[3, b].astype(F32) + in_l[3, b].astype(F32)
            w = idf_ref[pl.ds(b, 1), :]
            v = v * w
            st_ref[b] = v
            wt[b] = (v * w).astype(BF16)

        for k in range(SUB // SUBW):
            wgo(True, 1, sub * (SUB // SUBW) + k)
            wgo(False, 1, sub * (SUB // SUBW) + k)
    to_sibling(0)
    keep = pltpu.make_async_copy(wt, w_ref.at[mine], own_sem)
    keep.start()

    @pl.loop(0, 16)
    def _(b):
        v = st_ref[b]
        gram[...] += lax.dot_general(v, v, NT, precision=HIGH, preferred_element_type=F32)

    def side():
        for _ in gram_steps(
            at, gram, whole, half, from_sib, over_z, piece, over_xy, total, gram_sems
        ):
            yield
            yield
        yield from eliminate(terms, whole, linv_ref, work)

    aside = side()
    next(aside)
    order = (2, 3, 0, 1)
    for hop in (2, 3, 4):
        for n, sub in enumerate(order):
            wcopy(True, hop - 1, sub).wait_recv()
            if hop < 4 or sub < NW // 2:
                wgo(True, hop, sub)
            wcopy(False, hop - 1, sub).wait_recv()
            if hop < 4 or sub >= NW // 2:
                wgo(False, hop, sub)
            next(aside, None)
            next(aside, None)
        to_sibling(hop - 1)
        to_sibling(NZ - (hop - 1))
    for _ in aside:
        pass
    for sub in range(NW // 2):
        wcopy(True, 4, sub).wait_recv()
        wcopy(False, 4, sub + NW // 2).wait_recv()
    to_sibling(4)
    keep.wait()
    for c in passed:
        c.wait()
    for c in sent:
        c.wait_send()


def front(lists, tile_col, tiles, omega, idf, terms):
    dma = pltpu.SemaphoreType.DMA
    v = pltpu.VMEM
    return pl.pallas_call(
        functools.partial(front_kernel, terms),
        out_shape=(
            jax.ShapeDtypeStruct((16, 16, T, T), BF16),
            jax.ShapeDtypeStruct((16, T, T), F32),
            jax.ShapeDtypeStruct((T, T), F32),
        ),
        in_specs=[SMEM, SMEM, SMEM, SMEM, VMEM, VMEM, ANY],
        out_specs=(ANY, VMEM, VMEM),
        scratch_shapes=[
            v(tiles.shape, BF16),
            v((64, T, T), BF16),
            v((2 * PER, T, T), F32),
            v((2 * (PER + 1), T, T), F32),
            *[v((8, 16, T, T), BF16)] * 3,
            *[v((4, 16, T, T), BF16)] * 4,
            v((16, T, T), BF16),
            v((T, T), F32),
            v((T, T), F32),
            v((64, T), F32),
            v((64, T), F32),
            v((8, 8, T), F32),
            v((8, T), F32),
            v((16, 8, T), F32),
            v((64, T), F32),
            v((T, T), F32),
            dma,
            dma((10, 4)), dma((10, 4)),
            dma((8,)), dma((8,)),
            *[dma((4, 4))] * 4,
            dma,
            *[dma((4, NW))] * 4,
            dma((8,)), dma((8,)),
            dma, dma, dma((7,)), dma((7,)), dma((15,)), dma((15,)), dma((7,)), dma((7,)), dma, dma,
        ],
        compiler_params=params(54, 1),
        name="front",
    )(*lists, tile_col, omega, idf.reshape(16, T), tiles)


def project_kernel(col, group, slot, live, tiles_ref, w_ref, acc, raw, blocks, sem):
    step = pl.program_id(0)

    def fetch(step):
        at = step % 2
        copies = []
        for i in range(STEP):
            r = step * STEP + i
            copies.append(
                pltpu.make_async_copy(
                    w_ref.at[group[r] * 16 + slot[r]], blocks.at[at, i], sem.at[at, i]
                )
            )
        return copies

    @pl.when(step == 0)
    def _():
        for c in fetch(step):
            c.start()

    @pl.when(step + 1 < pl.num_programs(0))
    def _():
        for c in fetch(step + 1):
            c.start()

    @pl.when(step == 0)
    def _():
        @pl.loop(0, 64)
        def _(i):
            acc[i] = jnp.zeros((T, T), F32)

    for c in fetch(step):
        c.wait()
    for i in range(STEP):
        r = step * STEP + i
        tile_row = jnp.concatenate([tiles_ref[i, j] for j in range(5)], axis=1)
        w = blocks[step % 2, i]
        w = jnp.where(r < live[0], w, jnp.zeros_like(w))
        raw[i] = jnp.dot(w, tile_row, preferred_element_type=F32)
    for i in range(STEP):
        r = step * STEP + i
        for j in range(5):
            c = col[j, r]
            dev, b = c // 4, c % 4
            flow = b // 2
            u, v = dev // 4, dev % 4
            t = jnp.where(flow == 0, u * 4 + v, v * 4 + u)
            acc[flow * 32 + t * 2 + b % 2] += raw[i, :, j * T : (j + 1) * T]


def project(tiles, tile_col, strip_group, strip_slot, live_count, weighted):
    strips = tiles.shape[0]
    return pl.pallas_call(
        project_kernel,
        out_shape=jax.ShapeDtypeStruct((64, T, T), F32),
        grid=(strips // STEP,),
        in_specs=[
            SMEM,
            SMEM,
            SMEM,
            SMEM,
            pl.BlockSpec((STEP, 5, T, T), lambda i: (i, 0, 0, 0)),
            ANY,
        ],
        out_specs=pl.BlockSpec((64, T, T), lambda i: (0, 0, 0)),
        scratch_shapes=[
            pltpu.VMEM((STEP, T, 5 * T), F32),
            pltpu.VMEM((2, STEP, T, T), BF16),
            pltpu.SemaphoreType.DMA((2, STEP)),
        ],
        compiler_params=params(48),
        name="project",
    )(tile_col, strip_group, strip_slot, live_count, tiles, weighted.reshape(256, T, T))


def ring_sum(at, axis, own, out_refs, in_refs, send, recv, size):
    here = at[axis]
    dtype = out_refs[0].dtype
    low, high = pl.ds(0, size), pl.ds(size, size)
    r0, r1, l0, l1 = range(4)
    sent = []

    def copy(k, src, dst, right):
        return pltpu.make_async_remote_copy(
            src_ref=src,
            dst_ref=dst,
            send_sem=send.at[k],
            recv_sem=recv.at[k],
            device_id=moved(at, axis, 1 if right else -1, 4),
            device_id_type=MESH,
        )

    def fill(k, offset, target, extra=None):
        out = out_refs[k]
        base = 0 if k in (r0, l0) else offset

        @pl.loop(0, size)
        def _(b):
            v = own[target, b + offset]
            if extra is not None:
                v = v + extra[b].astype(F32)
            out[base + b] = v.astype(dtype)

    far = lax.rem(here + 2, 4)
    right, left = lax.rem(here + 1, 4), lax.rem(here + 3, 4)
    c_r0 = copy(0, out_refs[r0], in_refs[r0], True)
    c_l0 = copy(1, out_refs[l0], in_refs[l0], False)
    c_r1q = copy(2, out_refs[r1].at[high], in_refs[r1].at[high], True)
    c_l1p = copy(3, out_refs[l1].at[low], in_refs[l1].at[low], False)
    c_r1p = copy(4, out_refs[r1].at[low], in_refs[r1].at[low], True)
    c_l1q = copy(5, out_refs[l1].at[high], in_refs[l1].at[high], False)
    fill(r0, 0, far)
    c_r0.start()
    fill(l0, size, far)
    c_l0.start()
    yield
    fill(r1, size, right)
    c_r1q.start()
    fill(l1, 0, left)
    c_l1p.start()
    yield
    c_r0.wait_recv()
    fill(r1, 0, right, in_refs[r0])
    c_r1p.start()
    c_l0.wait_recv()
    fill(l1, size, left, in_refs[l0])
    c_l1q.start()
    yield
    for c in (c_r1q, c_l1p, c_r1p, c_l1q):
        c.wait_recv()
    yield
    for c in (c_r0, c_l0, c_r1q, c_l1p, c_r1p, c_l1q):
        c.wait_send()
    yield


def docs_kernel(part_ref, linv_ref, st_ref, out_ref, q_ref, *scratch):
    at = place()
    bufs1 = [scratch[0:8], scratch[8:16]]
    bufs2 = [scratch[16:24], scratch[24:32]]
    sums, final, send, recv = scratch[32:]
    greet([moved(at, "x", 1, 4), moved(at, "x", -1, 4), moved(at, "y", 1, 4), moved(at, "y", -1, 4)])
    axes = ("x", "y")
    runs = [
        ring_sum(
            at, axes[f], part_ref.at[f], bufs1[f][:4], bufs1[f][4:], send.at[f], recv.at[f], 4
        )
        for f in range(2)
    ]
    for _ in range(2):
        for run in runs:
            next(run)

    def basis(first, end):
        @pl.loop(first, end)
        def _(b):
            q_ref[pl.ds(b * T, T), :] = lax.dot_general(
                st_ref[b], linv_ref[...], (((0,), (1,)), ((), ())), precision=HIGH, preferred_element_type=F32
            )

    basis(0, 6)
    for run in runs:
        next(run)
    basis(6, 12)
    for run in runs:
        next(run)
    for f in range(2):
        in_r, in_l = bufs1[f][5], bufs1[f][7]
        here = at[axes[f]]

        @pl.loop(0, 8)
        def _(b):
            v = part_ref[f, here, b] + in_r[b].astype(F32) + in_l[b].astype(F32)
            sums[f, b // 2, b % 2] = v

    later = [
        ring_sum(
            at, axes[1 - f], sums.at[f], bufs2[f][:4], bufs2[f][4:], send.at[2 + f], recv.at[2 + f], 1
        )
        for f in range(2)
    ]
    for _ in range(2):
        for run in later:
            next(run)
    basis(12, 16)
    for _ in range(2):
        for run in later:
            next(run)
    for f in range(2):
        in_r, in_l = bufs2[f][5], bufs2[f][7]
        here = at[axes[1 - f]]
        for b in range(2):
            final[2 * f + b] = sums[f, here, b] + in_r[b].astype(F32) + in_l[b].astype(F32)
    for b in range(4):
        out_ref[:, b * T : (b + 1) * T] = jnp.dot(
            linv_ref[...], final[b], precision=HIGH, preferred_element_type=F32
        ).astype(BF16)
    for run in (*runs, *later):
        next(run)


def sum_docs(parts, linv, st):
    dma = pltpu.SemaphoreType.DMA

    def bufs(size, dtype):
        return [pltpu.VMEM((n * size, T, T), dtype) for n in (1, 2, 1, 2)] * 2

    return pl.pallas_call(
        docs_kernel,
        out_shape=(
            jax.ShapeDtypeStruct((T, 4 * T), BF16),
            jax.ShapeDtypeStruct((16 * T, T), F32),
        ),
        in_specs=[VMEM, VMEM, VMEM],
        out_specs=(VMEM, VMEM),
        scratch_shapes=[
            *bufs(4, BF16),
            *bufs(4, BF16),
            *bufs(1, BF16),
            *bufs(1, BF16),
            pltpu.VMEM((2, 4, 2, T, T), F32),
            pltpu.VMEM((4, T, T), F32),
            dma((4, 6)),
            dma((4, 6)),
        ],
        compiler_params=params(24, 4),
        name="docs_sum",
    )(parts.reshape(2, 4, 8, T, T), linv, st)


def on_device(tiles, tile_col, strip_group, strip_slot, live_count, omega, idf):
    terms = idf.shape[0] * 256
    lists = strip_lists(strip_group, strip_slot, live_count)
    tile_col = tile_col.T
    weighted, st, linv = front(lists, tile_col, tiles, omega, idf, terms)
    where = (tile_col, strip_group, strip_slot, live_count)
    doc_parts = project(tiles, *where, weighted)
    doc_factor, q_basis = sum_docs(doc_parts, linv, st)
    return q_basis, doc_factor


def solution(mesh):
    torus = Mesh(mesh.devices.reshape(8, 2, 4, 4), AXES)
    in_specs = (
        P(AXES, None, None, None),
        P(AXES, None),
        P(AXES),
        P(AXES),
        P(AXES),
        P(AXES, None),
        P(AXES),
    )
    out_specs = (P(AXES, None), P(None, AXES))
    return jax.shard_map(
        on_device, mesh=torus, in_specs=in_specs, out_specs=out_specs, check_vma=False
    )
```
